32 devices in a mesh: sub: 16 (over z, y, x), front: 2 (over core).
Axes of the slice: x: 2, y: 2, z: 4, core: 2. Of those that a mesh axis runs over, the one named last changes fastest.
Arguments:
- piv_cols: bfloat16 [16, 3072, 1024], P('sub', None, 'front'), may hold values from -6 to 6
- trail_cols: bfloat16 [16, 3072, 2048], P('sub', None, 'front'), may hold values from -6 to 6
- row_end: int32 [16, 24], P('sub'), may hold values from 128 to 3072, as said below
- parent_of: int32 [16], P('sub'), may hold values from 0 to 1, as said below
Outputs:
- r_pivot: float32 [2, 1024, 1024], P(None, None, 'front')
- r_trail: float32 [2, 1024, 2048], P(None, None, 'front')
The draws below stay inside these ranges and needn't reach their ends.
Inputs may be any that keep to these rules, and one draw needn't show every extreme that they name: row_end[c, j] is a multiple of 128 and never falls as j grows; in the column blocks j < 8 it is at most 1280, and it reaches 1280 for some child in every draw. `parent_of`: exactly 8 children have each parent.
All inputs are finite; a program needn't handle non-finite values.
Results may differ from the reference program's by a relative error of at most 0.0003.
Values may be sent and summed in bfloat16 or wider, within the bound.
No kernel may reach another device: no remote copies, remote signals or barrier semaphores. Data moves between devices by JAX's collectives and lax.ppermute only.
A program may use at most 128 MiB of HBM per device.

```python
import jax
import jax.numpy as jnp
from jax import lax

W = 3072
BLK = 128
KROWS = 3072
NPAR = 2
KIDS = 16
PIV = 1024
NB = 24


def draw_row_end(key, part):
    jumps = jax.random.randint(key, (KIDS, NB), 0, 3)
    chosen = jax.random.randint(jax.random.fold_in(key, 7), (), 0, KIDS)
    columns = jnp.arange(NB, dtype=jnp.int32)
    force = (jnp.arange(KIDS, dtype=jnp.int32)[:, None] == chosen) & (columns[None, :] == PIV // BLK - 1)
    jumps = jnp.where(force, 2, jumps)
    reach = lax.cummax(columns[None, :] + 1 + jumps, axis=1)
    return (BLK * jnp.minimum(reach, KROWS // BLK)).astype(jnp.int32)


def draw_parent_of(key, part):
    return (jax.random.permutation(key, KIDS) % NPAR).astype(jnp.int32)


def block_scale(own_key, extent, split, smallest, largest):
    level, own = 1.0, jax.random.fold_in(own_key, 6)
    for dim, parts in split:
        steps = jnp.exp(jax.random.uniform(jax.random.fold_in(own, dim), (parts,), jnp.float32, smallest / len(split), largest / len(split)))
        level = level * jnp.repeat(steps, extent[dim] // parts).reshape([-1 if axis == dim else 1 for axis in range(len(extent))])
    return level


def normal_values(key, shape, deviation, bound, pieces=(), kind=jnp.bfloat16):
    loudness = block_scale(key, shape, pieces, -0.22, 0.18) if pieces else 1.0
    array = jax.random.normal(key, shape, jnp.float32) * deviation * loudness
    return jnp.minimum(jnp.maximum(array, -bound), bound).astype(kind)


def setup_inputs(seed: int = 0) -> dict:
    keys = jax.random.split(jax.random.key(seed), 5)
    return {
        "piv_cols": normal_values(keys[0], (KIDS, KROWS, PIV), 1.0, 6.0, ((0, 16), (2, 2))),
        "trail_cols": normal_values(keys[1], (KIDS, KROWS, W - PIV), 1.0, 6.0, ((0, 16), (2, 2))),
        "row_end": draw_row_end(jax.random.fold_in(keys[4], 71), 0),
        "parent_of": draw_parent_of(jax.random.fold_in(keys[4], 71), 0),
    }


def reference(piv_cols, trail_cols, row_end, parent_of):
    row_ids = jnp.arange(KROWS, dtype=jnp.int32)[:, None]
    piv_block = (jnp.arange(PIV, dtype=jnp.int32) // BLK).astype(jnp.int32)
    trail_block = ((PIV + jnp.arange(W - PIV, dtype=jnp.int32)) // BLK).astype(jnp.int32)
    parent_ids = jnp.arange(NPAR, dtype=jnp.int32)

    def add_child(total, item):
        pivot, trail, stair_ends, parent = item
        live_pivot = row_ids < stair_ends[piv_block][None, :]
        live_trail = row_ids < stair_ends[trail_block][None, :]
        pivot = jnp.where(live_pivot, pivot, jnp.zeros((), pivot.dtype))
        trail = jnp.where(live_trail, trail, jnp.zeros((), trail.dtype))
        whole = jnp.concatenate([pivot, trail], axis=1)
        gram = jnp.dot(pivot.T.astype(jnp.float32), whole.astype(jnp.float32), preferred_element_type=jnp.float32)
        parent_pick = (parent_ids == parent).astype(jnp.float32)
        return (total + parent_pick[:, None, None] * gram[None], None)
    start = jnp.zeros((NPAR, PIV, W), jnp.float32)
    total, _ = lax.scan(add_child, start, (piv_cols, trail_cols, row_end, parent_of))
    factor_lower = jnp.linalg.cholesky(total[:, :, :PIV])
    r_pivot = jnp.transpose(factor_lower, (0, 2, 1))
    r_trail = lax.linalg.triangular_solve(factor_lower, total[:, :, PIV:], left_side=True, lower=True)
    return (r_pivot, r_trail)
```

```python
import jax, jax.numpy as jnp
from jax import lax
from jax.experimental import pallas as pl
from jax.experimental.pallas import tpu as pltpu
from jax.sharding import PartitionSpec as P
B=128
F32=jnp.float32
BF=jnp.bfloat16

def split(x):
    hi = x.astype(BF)
    return hi, (x - hi.astype(F32)).astype(BF)

def dot3(lhs, rhs):
    lh, ll = lhs
    rh, rl = rhs
    return jnp.dot(jnp.concatenate([lh, lh, ll], axis=1), jnp.concatenate([rh, rl, rh], axis=0), preferred_element_type=F32)

def factor_block(d_ref, w_ref, fillers):
    rows8 = (8, B)
    for g in range(B // 8):
        xs, xi = [], []
        for i in range(8):
            row = d_ref[8*g+i:8*g+i+1, :]
            xs.append(jnp.broadcast_to(row[:, :B], rows8))
            xi.append(jnp.broadcast_to(row[:, B:], rows8))
        s = {}
        for i in range(8):
            for j in range(i, 8):
                s[i, j] = jnp.broadcast_to(xs[i][:, 8*g+j:8*g+j+1], rows8)
        for i in range(8):
            rs = lax.rsqrt(s[i, i])
            inv = rs * rs
            w_ref[8*g+i:8*g+i+1, :B] = (xs[i] * rs)[:1]
            w_ref[8*g+i:8*g+i+1, B:] = (xi[i] * rs)[:1]
            for r in range(8):
                if r == i: continue
                m = (s[r, i] if r < i else s[i, r]) * inv
                for j in range(max(r, i+1), 8):
                    s[r, j] = s[r, j] - m * s[i, j]
                xs[r] = xs[r] - m * xs[i]
                xi[r] = xi[r] - m * xi[i]
            s[i, i] = inv
        ys = [xs[i] * s[i, i] for i in range(8)]
        yi = [xi[i] * s[i, i] for i in range(8)]
        for r in range(g+1, B // 8):
            blk = d_ref[8*r:8*r+8, :B]
            bi = d_ref[8*r:8*r+8, B:]
            cols = [jnp.broadcast_to(blk[:, 8*g+i:8*g+i+1], rows8) for i in range(8)]
            for i in range(8):
                blk = blk - cols[i] * ys[i]
                bi = bi - cols[i] * yi[i]
            d_ref[8*r:8*r+8, :B] = blk
            d_ref[8*r:8*r+8, B:] = bi
        if fillers:
            fillers.pop(0)()
    while fillers:
        fillers.pop(0)()

def chol_kernel(g_ref, t_ref, r_ref, z_ref, s_ref, d_ref, w_ref, rhs_ref):
    n = g_ref.shape[0]
    nt = t_ref.shape[1]
    nb = n // B
    ri = lax.broadcasted_iota(jnp.int32, (B, B), 0)
    ci = lax.broadcasted_iota(jnp.int32, (B, B), 1)
    def src(k, lo, hi):
        return s_ref[k*B:(k+1)*B, lo:hi]
    def update(k, i):
        def run():
            lo = i * B
            lhs = split(jnp.transpose(r_ref[k*B:(k+1)*B, lo:lo+B]))
            lhs = jnp.concatenate([lhs[0], lhs[0], lhs[1]], axis=1)
            upd = jnp.dot(lhs, rhs_ref[k % 2, :, lo:], preferred_element_type=F32)
            if k == 0:
                s_ref[lo:lo+B, lo:n] = g_ref[lo:lo+B, lo:n] - upd[:, :n-lo]
                s_ref[lo:lo+B, n:] = t_ref[lo:lo+B, :] - upd[:, n-lo:]
            else:
                s_ref[lo:lo+B, lo:] = s_ref[lo:lo+B, lo:] - upd
        return run
    fillers = []
    for k in range(nb):
        lo = k * B
        d_ref[:, :B] = g_ref[:B, :B] if k == 0 else s_ref[lo:lo+B, lo:lo+B]
        d_ref[:, B:] = jnp.where(ri == ci, 1.0, 0.0).astype(F32)
        factor_block(d_ref, w_ref, fillers)
        fillers = []
        if k:
            r_ref[lo:lo+B, :lo] = jnp.zeros((B, lo), F32)
        r_ref[lo:lo+B, lo:lo+B] = jnp.where(ci >= ri, w_ref[:, :B], 0.0)
        wh, wl = split(w_ref[:, B:])
        w3 = jnp.concatenate([wh, wh, wl], axis=1)
        if k < nb - 1:
            rest = g_ref[:B, B:] if k == 0 else s_ref[lo:lo+B, lo+B:n]
            rh, rl = split(rest)
            p = jnp.dot(w3, jnp.concatenate([rh, rl, rh], axis=0), preferred_element_type=F32)
            r_ref[lo:lo+B, lo+B:] = p
            ph, pll = split(p)
            rhs_ref[k % 2, 0:B, lo+B:n] = ph
            rhs_ref[k % 2, B:2*B, lo+B:n] = pll
            rhs_ref[k % 2, 2*B:, lo+B:n] = ph
        rest = t_ref[:B, :] if k == 0 else s_ref[lo:lo+B, n:]
        rh, rl = split(rest)
        p = jnp.dot(w3, jnp.concatenate([rh, rl, rh], axis=0), preferred_element_type=F32)
        z_ref[lo:lo+B, :] = p
        ph, pll = split(p)
        rhs_ref[k % 2, 0:B, n:] = ph
        rhs_ref[k % 2, B:2*B, n:] = pll
        rhs_ref[k % 2, 2*B:, n:] = ph
        if k < nb - 1:
            update(k, k+1)()
            fillers = [update(k, i) for i in range(k+2, nb)]

def chol_solve(g, t):
    n, nt = g.shape[0], t.shape[1]
    return pl.pallas_call(
        chol_kernel,
        out_shape=(jax.ShapeDtypeStruct((n, n), F32), jax.ShapeDtypeStruct((n, nt), F32)),
        in_specs=[pl.BlockSpec(memory_space=pltpu.VMEM)]*2,
        out_specs=(pl.BlockSpec(memory_space=pltpu.VMEM),)*2,
        scratch_shapes=[pltpu.VMEM((n, n+nt), F32), pltpu.VMEM((B, 2*B), F32), pltpu.VMEM((B, 2*B), F32), pltpu.VMEM((2, 3*B, n+nt), BF)],
        compiler_params=pltpu.CompilerParams(vmem_limit_bytes=40*1024*1024),
        cost_estimate=pl.CostEstimate(flops=3*n*n*n, bytes_accessed=4*n*(2*n+2*nt), transcendentals=0),
    )(g, t)

LIVE = 1280
NPAR = 2


def owned_ends(stair_ends, first, count):
    blocks = (first + jnp.arange(count, dtype=jnp.int32)) // B
    table = blocks[:, None] == jnp.arange(stair_ends.shape[0], dtype=jnp.int32)[None, :]
    return jnp.sum(jnp.where(table, stair_ends[None, :], 0), axis=1)


def swap_front(mine0, mine1, position, axis):
    keep = jnp.where(position == 0, mine0, mine1)
    give = jnp.where(position == 0, mine1, mine0)
    got = lax.ppermute(give, "front", [(0, 1), (1, 0)])
    first = jnp.where(position == 0, keep, got)
    second = jnp.where(position == 0, got, keep)
    return jnp.concatenate([first, second], axis=axis)


def shards(piv_cols, trail_cols, row_end, parent_of):
    position = lax.axis_index("front")
    tile_pivot = piv_cols.shape[2]
    tile_trail = trail_cols.shape[2]
    pivot_total = tile_pivot * lax.axis_size("front")
    stair_ends = row_end[0]
    row_ids = jnp.arange(LIVE, dtype=jnp.int32)[:, None]
    end_pivot = owned_ends(stair_ends, position * tile_pivot, tile_pivot)
    end_trail = owned_ends(stair_ends, pivot_total + position * tile_trail, tile_trail)
    pivot = jnp.where(row_ids < end_pivot[None, :], piv_cols[0, :LIVE], jnp.zeros((), piv_cols.dtype))
    trail = jnp.where(row_ids < end_trail[None, :], trail_cols[0, :LIVE], jnp.zeros((), trail_cols.dtype))
    own_columns = jnp.concatenate([pivot, trail], axis=1)
    gram = jnp.einsum("rk,rt->kt", lax.all_gather(pivot, "front", axis=1, tiled=True), own_columns, preferred_element_type=F32)
    parent_pick = (jnp.arange(NPAR, dtype=jnp.int32) == parent_of[0]).astype(F32)
    slots = parent_pick[:, None, None] * gram[None]
    pivot_part = lax.psum(slots[:, :, :tile_pivot], "sub")
    trail_part = lax.psum_scatter(slots[:, :, tile_pivot:], "sub", scatter_dimension=2, tiled=True)
    pivot_own = swap_front(pivot_part[0], pivot_part[1], position, 1)
    trail_own = swap_front(trail_part[0], trail_part[1], position, 1)
    factor, solved = chol_solve(pivot_own, trail_own)
    share = solved.shape[1] // 2
    solved_share = swap_front(solved[:, :share], solved[:, share:], position, 0).reshape(NPAR, solved.shape[0], share)
    r_pivot = swap_front(factor[:, :tile_pivot], factor[:, tile_pivot:], position, 0).reshape(NPAR, factor.shape[0], tile_pivot)
    r_trail = lax.all_gather(solved_share, "sub", axis=2, tiled=True)
    return (r_pivot, r_trail)


def solution(mesh):
    return jax.shard_map(
        shards,
        mesh=mesh,
        in_specs=(P("sub", None, "front"), P("sub", None, "front"), P("sub", None), P("sub")),
        out_specs=(P(None, None, "front"), P(None, None, "front")),
        check_vma=False,
    )
```

```python
import jax, jax.numpy as jnp
from jax import lax
from jax.experimental import pallas as pl
from jax.experimental.pallas import tpu as pltpu
from jax.sharding import PartitionSpec as P
B=128
F32=jnp.float32
BF=jnp.bfloat16
LIVE = 1280
NPAR = 2
PIECES = 4
LEVELS = 32766.0

def split(x):
    hi = x.astype(BF)
    return hi, (x - hi.astype(F32)).astype(BF)

def factor_block(d_ref, w_ref, fillers):
    rows8 = (8, B)
    for g in range(B // 8):
        xs, xi = [], []
        for i in range(8):
            row = d_ref[8*g+i:8*g+i+1, :]
            xs.append(jnp.broadcast_to(row[:, :B], rows8))
            xi.append(jnp.broadcast_to(row[:, B:], rows8))
        s = {}
        for i in range(8):
            for j in range(i, 8):
                s[i, j] = jnp.broadcast_to(xs[i][:, 8*g+j:8*g+j+1], rows8)
        for i in range(8):
            rs = lax.rsqrt(s[i, i])
            inv = rs * rs
            w_ref[8*g+i:8*g+i+1, :B] = (xs[i] * rs)[:1]
            w_ref[8*g+i:8*g+i+1, B:] = (xi[i] * rs)[:1]
            for r in range(8):
                if r == i: continue
                m = (s[r, i] if r < i else s[i, r]) * inv
                for j in range(max(r, i+1), 8):
                    s[r, j] = s[r, j] - m * s[i, j]
                xs[r] = xs[r] - m * xs[i]
                xi[r] = xi[r] - m * xi[i]
            s[i, i] = inv
        ys = [xs[i] * s[i, i] for i in range(8)]
        yi = [xi[i] * s[i, i] for i in range(8)]
        for r in range(g+1, B // 8):
            blk = d_ref[8*r:8*r+8, :B]
            bi = d_ref[8*r:8*r+8, B:]
            cols = [jnp.broadcast_to(blk[:, 8*g+i:8*g+i+1], rows8) for i in range(8)]
            for i in range(8):
                blk = blk - cols[i] * ys[i]
                bi = bi - cols[i] * yi[i]
            d_ref[8*r:8*r+8, :B] = blk
            d_ref[8*r:8*r+8, B:] = bi
        if fillers:
            fillers.pop(0)()
    while fillers:
        fillers.pop(0)()


def tri_index(i, j, nb):
    return i * nb - i * (i - 1) // 2 + (j - i)


def chol_kernel(g_ref, t_ref, r_ref, q_ref, s_ref, z_ref, d_ref, w_ref, rhs_ref):
    n = t_ref.shape[1]
    nt = t_ref.shape[0]
    nb = n // B
    ri = lax.broadcasted_iota(jnp.int32, (B, B), 0)
    ci = lax.broadcasted_iota(jnp.int32, (B, B), 1)

    def gram_block(i, j):
        at = tri_index(i, j, nb) * B
        return g_ref[at:at+B, :]

    def update(k, i):
        def run():
            lo = i * B
            lhs = split(jnp.transpose(r_ref[k*B:(k+1)*B, lo:lo+B]))
            lhs = jnp.concatenate([lhs[0], lhs[0], lhs[1]], axis=1)
            upd = jnp.dot(lhs, rhs_ref[k % 2, :, lo:], preferred_element_type=F32)
            if k == 0:
                for j in range(i, nb):
                    s_ref[lo:lo+B, j*B:(j+1)*B] = gram_block(i, j) - upd[:, (j-i)*B:(j-i+1)*B]
                s_ref[lo:lo+B, n:] = jnp.transpose(t_ref[:, lo:lo+B]) - upd[:, n-lo:]
            else:
                s_ref[lo:lo+B, lo:] = s_ref[lo:lo+B, lo:] - upd
        return run

    fillers = []
    for k in range(nb):
        lo = k * B
        d_ref[:, :B] = gram_block(0, 0) if k == 0 else s_ref[lo:lo+B, lo:lo+B]
        d_ref[:, B:] = jnp.where(ri == ci, 1.0, 0.0).astype(F32)
        factor_block(d_ref, w_ref, fillers)
        fillers = []
        if k:
            r_ref[lo:lo+B, :lo] = jnp.zeros((B, lo), F32)
        r_ref[lo:lo+B, lo:lo+B] = jnp.where(ci >= ri, w_ref[:, :B], 0.0)
        wh, wl = split(w_ref[:, B:])
        w3 = jnp.concatenate([wh, wh, wl], axis=1)
        if k < nb - 1:
            rest = g_ref[B:nb*B, :] if k == 0 else s_ref[lo:lo+B, lo+B:n]
            if k == 0:
                rest = jnp.concatenate([gram_block(0, j) for j in range(1, nb)], axis=1)
            rh, rl = split(rest)
            p = jnp.dot(w3, jnp.concatenate([rh, rl, rh], axis=0), preferred_element_type=F32)
            r_ref[lo:lo+B, lo+B:] = p
            ph, pll = split(p)
            rhs_ref[k % 2, 0:B, lo+B:n] = ph
            rhs_ref[k % 2, B:2*B, lo+B:n] = pll
            rhs_ref[k % 2, 2*B:, lo+B:n] = ph
        rest = jnp.transpose(t_ref[:, :B]) if k == 0 else s_ref[lo:lo+B, n:]
        rh, rl = split(rest)
        p = jnp.dot(w3, jnp.concatenate([rh, rl, rh], axis=0), preferred_element_type=F32)
        z_ref[lo:lo+B, :] = p
        ph, pll = split(p)
        rhs_ref[k % 2, 0:B, n:] = ph
        rhs_ref[k % 2, B:2*B, n:] = pll
        rhs_ref[k % 2, 2*B:, n:] = ph
        if k < nb - 1:
            update(k, k+1)()
            fillers = [update(k, i) for i in range(k+2, nb)]
    exps, mants = [], []
    for k in range(nb):
        z = z_ref[k*B:(k+1)*B, :]
        top = jnp.maximum(jnp.max(jnp.abs(z), axis=0, keepdims=True), 1e-30)
        e = jnp.ceil(jnp.log2(top))
        mant = jnp.minimum(jnp.ceil(top * jnp.exp2(-e) * 16384.0) + 1.0, 32767.0)
        step = mant * jnp.exp2(e) * (1.0 / (16384.0 * LEVELS))
        codes = jnp.clip(jnp.round(z * (1.0 / step)), -LEVELS, LEVELS)
        q_ref[k*B:(k+1)*B, :] = codes.astype(jnp.int32).astype(jnp.int16)
        exps.append(e)
        mants.append(mant)
    q_ref[n:, :] = jnp.concatenate(exps + mants, axis=0).astype(jnp.int32).astype(jnp.int16)


def chol_solve(g, t):
    nt, n = t.shape
    vmem = pl.BlockSpec(memory_space=pltpu.VMEM)
    return pl.pallas_call(
        chol_kernel,
        out_shape=(jax.ShapeDtypeStruct((n, n), F32), jax.ShapeDtypeStruct((n + 2 * (n // B), nt), jnp.int16)),
        in_specs=[vmem] * 2,
        out_specs=(vmem,) * 2,
        scratch_shapes=[
            pltpu.VMEM((n, n + nt), F32),
            pltpu.VMEM((n, nt), F32),
            pltpu.VMEM((B, 2*B), F32),
            pltpu.VMEM((B, 2*B), F32),
            pltpu.VMEM((2, 3*B, n + nt), BF),
        ],
        compiler_params=pltpu.CompilerParams(vmem_limit_bytes=40*1024*1024),
        cost_estimate=pl.CostEstimate(flops=3*n*n*n, bytes_accessed=4*n*(2*n+2*nt), transcendentals=0),
    )(g, t)


def gram_kernel(info_ref, own_ref, other_ref, trail_ref, g_ref, *rest):
    t_refs, a_ref = rest[:-1], rest[-1]
    nb_all = info_ref.shape[0] - 2
    live, tile = other_ref.shape
    n = a_ref.shape[1]
    nb = n // B
    place = info_ref[nb_all + 1]
    wanted = info_ref[nb_all] == place
    rows = lax.broadcasted_iota(jnp.int32, (live, B), 0)
    zero = jnp.zeros((live, B), BF)
    per = tile // B
    for half, ref in ((place, own_ref.at[0]), (1 - place, other_ref)):
        for j in range(per):
            end = info_ref[half * per + j]
            at = pl.multiple_of(half * tile + j * B, B)
            a_ref[:, pl.ds(at, B)] = jnp.where(rows < end, ref[:, j*B:(j+1)*B], zero)
    dims = (((0,), (0,)), ((), ()))

    @pl.when(wanted)
    def _():
        for i in range(0, nb, 2):
            lhs = a_ref[:, i*B:(i+2)*B]
            out = lax.dot_general(lhs, a_ref[:, i*B:], dims, preferred_element_type=F32)
            for r in (i, i + 1):
                for j in range(r, nb):
                    at = tri_index(r, j, nb) * B
                    g_ref[at:at+B, :] = out[(r-i)*B:(r-i+1)*B, (j-i)*B:(j-i+1)*B]

    @pl.when(jnp.logical_not(wanted))
    def _():
        g_ref[...] = jnp.zeros(g_ref.shape, F32)

    trail_tile = trail_ref.shape[2]
    trail_per = trail_tile // B
    piece = t_refs[0].shape[1]
    for j in range(0, trail_per, 2):
        cols = []
        for h in (j, j + 1):
            end = info_ref[nb + place * trail_per + h]
            cols.append(jnp.where(rows < end, trail_ref[0, :, h*B:(h+1)*B], zero))
        out = lax.dot_general(jnp.concatenate(cols, axis=1), a_ref[...], dims, preferred_element_type=F32)
        for q, t_ref in enumerate(t_refs):
            t_ref[j*B:(j+2)*B, :] = out[:, q*piece:(q+1)*piece]


def grams(info, piv, other, trail, pieces):
    live, tile = other.shape
    n = 2 * tile
    nb = n // B
    wide = trail.shape[2]
    packed = nb * (nb + 1) // 2 * B
    first = lambda i, info: (0, 0, 0)
    flat = lambda i, info: (0, 0)
    return pl.pallas_call(
        gram_kernel,
        out_shape=(jax.ShapeDtypeStruct((packed, B), F32),) + (jax.ShapeDtypeStruct((wide, n // pieces), F32),) * pieces,
        grid_spec=pltpu.PrefetchScalarGridSpec(
            num_scalar_prefetch=1,
            grid=(1,),
            in_specs=[
                pl.BlockSpec((1, live, tile), first),
                pl.BlockSpec((live, tile), flat),
                pl.BlockSpec((1, live, wide), first),
            ],
            out_specs=(pl.BlockSpec((packed, B), flat),) + (pl.BlockSpec((wide, n // pieces), flat),) * pieces,
            scratch_shapes=[pltpu.VMEM((live, n), BF)],
        ),
        compiler_params=pltpu.CompilerParams(vmem_limit_bytes=48*1024*1024),
        cost_estimate=pl.CostEstimate(flops=2*live*n*(wide+n//2), bytes_accessed=2*live*(n+wide)+4*n*(wide+n//2), transcendentals=0),
    )(info, piv, other, trail)


def unpack_kernel(q_ref, s_ref, o_ref):
    chips, rows, lanes = q_ref.shape
    nb = s_ref.shape[1] // 2
    half = lanes // 2
    lane = lax.broadcasted_iota(jnp.int32, (rows, lanes), 1)
    which = lax.broadcasted_iota(jnp.int32, (nb, lanes), 0) == pl.program_id(0)

    def values(c):
        sc = s_ref[c].astype(jnp.int32).astype(F32)
        step = sc[nb:] * jnp.exp2(sc[:nb]) * (1.0 / (16384.0 * LEVELS))
        step = jnp.sum(jnp.where(which, step, 0.0), axis=0, keepdims=True)
        return q_ref[c].astype(jnp.int32).astype(F32) * step

    for c in range(0, chips, 2):
        a, b = values(c), values(c + 1)
        at = c * half
        o_ref[0, :, at:at+lanes] = jnp.where(lane < half, a, pltpu.roll(b, half, 1))
        o_ref[1, :, at:at+lanes] = jnp.where(lane < half, pltpu.roll(a, half, 1), b)


def unpack(q, n):
    chips, rows, lanes = q.shape
    wide = chips * lanes // 2
    nb = n // B
    return pl.pallas_call(
        unpack_kernel,
        out_shape=jax.ShapeDtypeStruct((NPAR, n, wide), F32),
        grid=(nb,),
        in_specs=[pl.BlockSpec((chips, B, lanes), lambda k: (0, k, 0)), pl.BlockSpec((chips, 2 * nb, lanes), lambda k: (0, n // (2 * nb), 0))],
        out_specs=pl.BlockSpec((NPAR, B, wide), lambda k: (0, k, 0)),
        compiler_params=pltpu.CompilerParams(vmem_limit_bytes=40*1024*1024),
        cost_estimate=pl.CostEstimate(flops=0, bytes_accessed=2*q.size+8*n*wide, transcendentals=0),
    )(q, q)


def unpack_plain(q, n):
    chips, rows, lanes = q.shape
    nb = n // B
    sc = q[:, n:].astype(F32)
    step = sc[:, nb:] * jnp.exp2(sc[:, :nb]) * (1.0 / (16384.0 * LEVELS))
    z = q[:, :n].astype(F32).reshape(chips, nb, B, lanes) * step[:, :, None, :]
    z = z.reshape(chips, n, NPAR, lanes // NPAR)
    return jnp.transpose(z, (2, 1, 0, 3)).reshape(NPAR, n, chips * lanes // NPAR)


def take(x, axis, index):
    return lax.dynamic_index_in_dim(x, index, axis, keepdims=False)


def flip(x, bit, count):
    return lax.ppermute(x, "sub", [(i, i ^ bit) for i in range(count)])


def halve(x, axis, bit, me, count):
    own = jnp.where(me & bit, 1, 0)
    return take(x, axis, own) + flip(take(x, axis, 1 - own), bit, count)


def bit_orders(count):
    bits = [1 << i for i in range(count.bit_length() - 1)]
    plane = len(bits) // 2
    other = bits[:plane][::-1] + bits[plane:]
    return bits, other


def sum_everywhere(x, order, me, count):
    steps = len(order)
    x = x.reshape((2,) * steps + x.shape[1:])
    for bit in order:
        x = halve(x, 0, bit, me, count)
    for bit in order[::-1]:
        other = flip(x, bit, count)
        up = (me & bit) != 0
        x = jnp.stack([jnp.where(up, other, x), jnp.where(up, x, other)])
    return x.reshape((count,) + x.shape[steps:])


def sum_shares(x, order, me, count, parent, partner):
    left = [1 << i for i in range(count.bit_length() - 1)][::-1]
    x = x.reshape((2,) * len(left) + (x.shape[0] // count, x.shape[1]))
    bit = order[0]
    axis = left.index(bit)
    own = jnp.where(me & bit, 1, 0)
    got = flip(take(x, axis, 1 - own), bit, count)
    kept = take(x, axis, own)
    left.remove(bit)
    x = jnp.stack([jnp.where(parent == p, kept, 0.0) + jnp.where(partner == p, got, 0.0) for p in range(NPAR)])
    for bit in order[1:]:
        x = halve(x, 1 + left.index(bit), bit, me, count)
        left.remove(bit)
    return x


def shards(count, piv_cols, trail_cols, row_end, parent_of):
    place = lax.axis_index("front")
    me = lax.axis_index("sub")
    swap = [(0, 1), (1, 0)]
    tile_pivot = piv_cols.shape[2]
    n = NPAR * tile_pivot
    orders = bit_orders(count)
    other_piv = lax.ppermute(piv_cols[0, :LIVE], "front", swap)
    parent = parent_of[0]
    partners = [flip(parent_of, order[0], count)[0] for order in orders]
    info = jnp.concatenate([row_end[0], parent_of, place[None].astype(jnp.int32)])
    packed, *trails = grams(info, piv_cols, other_piv, trail_cols, PIECES)

    packed = packed.reshape(count, packed.shape[0] // count, B)
    cut = packed.shape[1] // 2
    parts = [sum_everywhere(part, order, me, count) for part, order in zip((packed[:, :cut], packed[:, cut:]), orders)]
    gram = jnp.concatenate(parts, axis=1).reshape(-1, B)

    shares = [sum_shares(t, orders[q % 2], me, count, parent, partners[q % 2]) for q, t in enumerate(trails)]
    share = jnp.concatenate(shares, axis=2)
    width = share.shape[1]
    keep = take(share, 0, place)
    got = lax.ppermute(take(share, 0, 1 - place), "front", swap)
    trail = jnp.concatenate([jnp.where(place == 0, keep, got), jnp.where(place == 0, got, keep)], axis=0)

    factor, codes = chol_solve(gram, trail)

    theirs = lax.ppermute(codes, "front", swap)
    packed_codes = jnp.where(
        place == 0,
        jnp.concatenate([codes[:, :width], theirs[:, :width]], axis=1),
        jnp.concatenate([theirs[:, width:], codes[:, width:]], axis=1),
    )
    every = lax.all_gather(packed_codes, "sub", axis=0)
    r_trail = unpack(every, n) if 2 * width == B else unpack_plain(every, n)

    low, high = factor[:, :tile_pivot], factor[:, tile_pivot:]
    keep = jnp.where(place == 0, low, high)
    got = lax.ppermute(jnp.where(place == 0, high, low), "front", swap)
    r_pivot = jnp.stack([jnp.where(place == 0, keep, got), jnp.where(place == 0, got, keep)])
    return (r_pivot, r_trail)


def solution(mesh):
    count = mesh.shape["sub"]
    return jax.shard_map(
        lambda *args: shards(count, *args),
        mesh=mesh,
        in_specs=(P("sub", None, "front"), P("sub", None, "front"), P("sub", None), P("sub")),
        out_specs=(P(None, None, "front"), P(None, None, "front")),
        check_vma=False,
    )
```

```python
import jax, jax.numpy as jnp
from jax import lax
from jax.experimental import pallas as pl
from jax.experimental.pallas import tpu as pltpu
from jax.sharding import PartitionSpec as P
B=128
F32=jnp.float32
BF=jnp.bfloat16
LIVE = 1280
NPAR = 2
PIECES = 4
LEVELS = 32766.0
SWAP = [(0, 1), (1, 0)]

def split(x):
    hi = x.astype(BF)
    return hi, (x - hi.astype(F32)).astype(BF)

def factor_block(d_ref, w_ref, fillers):
    rows8 = (8, B)
    for g in range(B // 8):
        xs, xi = [], []
        for i in range(8):
            row = d_ref[8*g+i:8*g+i+1, :]
            xs.append(jnp.broadcast_to(row[:, :B], rows8))
            xi.append(jnp.broadcast_to(row[:, B:], rows8))
        s = {}
        for i in range(8):
            for j in range(i, 8):
                s[i, j] = jnp.broadcast_to(xs[i][:, 8*g+j:8*g+j+1], rows8)
        for i in range(8):
            rs = lax.rsqrt(s[i, i])
            inv = rs * rs
            w_ref[8*g+i:8*g+i+1, :B] = (xs[i] * rs)[:1]
            w_ref[8*g+i:8*g+i+1, B:] = (xi[i] * rs)[:1]
            for r in range(8):
                if r == i: continue
                m = (s[r, i] if r < i else s[i, r]) * inv
                for j in range(max(r, i+1), 8):
                    s[r, j] = s[r, j] - m * s[i, j]
                xs[r] = xs[r] - m * xs[i]
                xi[r] = xi[r] - m * xi[i]
            s[i, i] = inv
        ys = [xs[i] * s[i, i] for i in range(8)]
        yi = [xi[i] * s[i, i] for i in range(8)]
        for r in range(g+1, B // 8):
            blk = d_ref[8*r:8*r+8, :B]
            bi = d_ref[8*r:8*r+8, B:]
            cols = [jnp.broadcast_to(blk[:, 8*g+i:8*g+i+1], rows8) for i in range(8)]
            for i in range(8):
                blk = blk - cols[i] * ys[i]
                bi = bi - cols[i] * yi[i]
            d_ref[8*r:8*r+8, :B] = blk
            d_ref[8*r:8*r+8, B:] = bi
        if fillers:
            fillers.pop(0)()
    while fillers:
        fillers.pop(0)()


def gram_rows(i, j):
    t = j // 2
    return j % 2, (t * t + t + i) * B


def chol_kernel(first, last, *refs):
    begin = first == 0
    if begin:
        g_ref, t_ref, *refs = refs
    else:
        in_ref, *refs = refs
    r_ref, q_ref, *refs = refs
    if begin:
        out_ref, *refs = refs
    s_ref, z_ref, d_ref, w_ref, rhs_ref = refs
    nt = z_ref.shape[1]
    n = r_ref.shape[1]
    nb = n // B
    base = first * B
    ri = lax.broadcasted_iota(jnp.int32, (B, B), 0)
    ci = lax.broadcasted_iota(jnp.int32, (B, B), 1)

    def gram_block(i, j):
        core, at = gram_rows(i, j)
        share = g_ref.shape[2]
        parts, end = [], at + B
        while at < end:
            chip, off = at // share, at % share
            size = min(share - off, end - at)
            parts.append(g_ref[chip, core, off:off+size, :])
            at += size
        return parts[0] if len(parts) == 1 else jnp.concatenate(parts, axis=0)

    def left(i, lo, hi):
        if not begin:
            return in_ref[(i-first)*B:(i-first+1)*B, lo-base:hi-base]
        if lo >= n:
            return jnp.transpose(t_ref[:, i*B:(i+1)*B])
        parts = [gram_block(i, j) for j in range(lo // B, min(hi, n) // B)]
        if hi > n:
            parts.append(jnp.transpose(t_ref[:, i*B:(i+1)*B]))
        return parts[0] if len(parts) == 1 else jnp.concatenate(parts, axis=1)

    def current(k, lo, hi):
        return left(k, lo, hi) if k == first else s_ref[k*B-base:(k+1)*B-base, lo-base:hi-base]

    def update(k, i):
        def run():
            lo = i * B
            lhs = split(jnp.transpose(r_ref[k*B-base:(k+1)*B-base, lo:lo+B]))
            lhs = jnp.concatenate([lhs[0], lhs[0], lhs[1]], axis=1)
            upd = jnp.dot(lhs, rhs_ref[k % 2, :, lo-base:], preferred_element_type=F32)
            new = current(i, lo, n + nt) - upd if k > first else left(i, lo, n + nt) - upd
            if i >= last and k == last - 1:
                out_ref[(i-last)*B:(i-last+1)*B, lo-last*B:] = new
            else:
                s_ref[lo-base:lo-base+B, lo-base:] = new
        return run

    fillers = []
    for k in range(first, last):
        lo = k * B
        at = lo - base
        d_ref[:, :B] = current(k, lo, lo + B)
        d_ref[:, B:] = jnp.where(ri == ci, 1.0, 0.0).astype(F32)
        factor_block(d_ref, w_ref, fillers)
        fillers = []
        if k:
            r_ref[at:at+B, :lo] = jnp.zeros((B, lo), F32)
        r_ref[at:at+B, lo:lo+B] = jnp.where(ci >= ri, w_ref[:, :B], 0.0)
        wh, wl = split(w_ref[:, B:])
        w3 = jnp.concatenate([wh, wh, wl], axis=1)
        rh, rl = split(current(k, lo + B, n + nt))
        p = jnp.dot(w3, jnp.concatenate([rh, rl, rh], axis=0), preferred_element_type=F32)
        if k < nb - 1:
            r_ref[at:at+B, lo+B:] = p[:, :n-lo-B]
        z_ref[at:at+B, :] = p[:, n-lo-B:]
        ph, pll = split(p)
        rhs_ref[k % 2, 0:B, lo+B-base:] = ph
        rhs_ref[k % 2, B:2*B, lo+B-base:] = pll
        rhs_ref[k % 2, 2*B:, lo+B-base:] = ph
        if k < nb - 1:
            update(k, k+1)()
            fillers = [update(k, i) for i in range(k+2, nb)]
    for fill in fillers:
        fill()
    count = last - first
    codes, scales = [], []
    for k in range(count):
        z = z_ref[k*B:(k+1)*B, :]
        top = jnp.maximum(jnp.max(jnp.abs(z), axis=0, keepdims=True), 1e-30)
        e = jnp.ceil(jnp.log2(top))
        mant = jnp.minimum(jnp.ceil(top * jnp.exp2(-e) * 16384.0) + 1.0, 32767.0)
        step = mant * jnp.exp2(e) * (1.0 / (16384.0 * LEVELS))
        codes.append(jnp.clip(jnp.round(z * (1.0 / step)), -LEVELS, LEVELS).astype(jnp.int32))
        scales.append(join(e.astype(jnp.int32), mant.astype(jnp.int32)))
    for k in range(count // 2):
        q_ref[k*B:(k+1)*B, :] = join(codes[k], codes[k + count // 2])
    scales += [jnp.zeros_like(scales[0])] * (8 - count)
    q_ref[count//2*B:, :] = jnp.concatenate(scales, axis=0)


def join(high, low):
    return jnp.bitwise_or(jnp.left_shift(high, 16), jnp.bitwise_and(low, 65535))


def high_low(word):
    return jnp.right_shift(word, 16), jnp.right_shift(jnp.left_shift(word, 16), 16)


def chol_rows(first, last, n, nt, *args):
    vmem = pl.BlockSpec(memory_space=pltpu.VMEM)
    rows = (last - first) * B
    wide = n + nt - first * B
    outs = [jax.ShapeDtypeStruct((rows, n), F32), jax.ShapeDtypeStruct((rows // 2 + 8, nt), jnp.int32)]
    if first == 0:
        outs.append(jax.ShapeDtypeStruct((n - last * B, n + nt - last * B), F32))
    return pl.pallas_call(
        lambda *refs: chol_kernel(first, last, *refs),
        out_shape=tuple(outs),
        in_specs=[vmem] * len(args),
        out_specs=(vmem,) * len(outs),
        scratch_shapes=[
            pltpu.VMEM((n - first * B, wide), F32),
            pltpu.VMEM((rows, nt), F32),
            pltpu.VMEM((B, 2*B), F32),
            pltpu.VMEM((B, 2*B), F32),
            pltpu.VMEM((2, 3*B, wide), BF),
        ],
        compiler_params=pltpu.CompilerParams(vmem_limit_bytes=40*1024*1024),
        cost_estimate=pl.CostEstimate(flops=30*n*n*n // 2, bytes_accessed=4*rows*n, transcendentals=0),
    )(*args)


DIMS = (((0,), (0,)), ((), ()))


def pivot_kernel(info_ref, own_ref, other_ref, g_ref, a_ref):
    live, tile = other_ref.shape
    n = a_ref.shape[1]
    place = info_ref[info_ref.shape[0] - 1]
    rows = lax.broadcasted_iota(jnp.int32, (live, B), 0)
    zero = jnp.zeros((live, B), BF)
    per = tile // B
    for half, ref in ((place, own_ref.at[0]), (1 - place, other_ref)):
        for j in range(per):
            end = info_ref[half * per + j]
            at = pl.multiple_of(half * tile + j * B, B)
            a_ref[:, pl.ds(at, B)] = jnp.where(rows < end, ref[:, j*B:(j+1)*B], zero)
    for t in range(n // B // 2):
        at = pl.multiple_of((2 * t + place) * B, B)
        out = lax.dot_general(a_ref[:, :(2*t+2)*B], a_ref[:, pl.ds(at, B)], DIMS, preferred_element_type=F32)
        g_ref[(t*t+t)*B:(t*t+3*t+2)*B, :] = out


def trail_kernel(info_ref, a_ref, trail_ref, *t_refs):
    live, n = a_ref.shape
    place = info_ref[info_ref.shape[0] - 1]
    rows = lax.broadcasted_iota(jnp.int32, (live, B), 0)
    zero = jnp.zeros((live, B), BF)
    per = trail_ref.shape[2] // B
    piece = t_refs[0].shape[1]
    for j in range(0, per, 2):
        cols = []
        for h in (j, j + 1):
            end = info_ref[n // B + place * per + h]
            cols.append(jnp.where(rows < end, trail_ref[0, :, h*B:(h+1)*B], zero))
        out = lax.dot_general(jnp.concatenate(cols, axis=1), a_ref[...], DIMS, preferred_element_type=F32)
        for q, t_ref in enumerate(t_refs):
            t_ref[j*B:(j+2)*B, :] = out[:, q*piece:(q+1)*piece]


def one_step(kernel, info, args, blocks, outs, cost):
    return pl.pallas_call(
        kernel,
        out_shape=tuple(outs),
        grid_spec=pltpu.PrefetchScalarGridSpec(
            num_scalar_prefetch=1,
            grid=(1,),
            in_specs=[pl.BlockSpec(block, lambda i, info, zeros=(0,) * len(block): zeros) for block in blocks],
            out_specs=tuple(pl.BlockSpec(out.shape, lambda i, info: (0, 0)) for out in outs),
        ),
        compiler_params=pltpu.CompilerParams(vmem_limit_bytes=40*1024*1024),
        cost_estimate=pl.CostEstimate(flops=cost, bytes_accessed=16*1024*1024, transcendentals=0),
    )(info, *args)


def pivot_gram(info, piv, other):
    live, tile = other.shape
    n = 2 * tile
    half = n // B // 2
    outs = [jax.ShapeDtypeStruct(((half * half + half) * B, B), F32), jax.ShapeDtypeStruct((live, n), BF)]
    return one_step(pivot_kernel, info, (piv, other), [(1, live, tile), (live, tile)], outs, live*n*n)


def trail_gram(info, masked, trail, pieces):
    live, n = masked.shape
    wide = trail.shape[2]
    outs = [jax.ShapeDtypeStruct((wide, n // pieces), F32)] * pieces
    return one_step(trail_kernel, info, (masked, trail), [(live, n), (1, live, wide)], outs, 2*live*n*wide)


def step_of(word):
    e, mant = high_low(word)
    return mant.astype(F32) * jnp.exp2(e.astype(F32)) * (1.0 / (16384.0 * LEVELS))


def unpack_kernel(q_ref, s_ref, *rest):
    o_ref = rest[-1]
    chips, rows, lanes = q_ref.shape
    half = lanes // 2
    lane = lax.broadcasted_iota(jnp.int32, (rows, lanes), 1)
    which = lax.broadcasted_iota(jnp.int32, (8, lanes), 0)
    blocks = pl.num_programs(0)

    def values(c):
        steps = step_of(s_ref[c])
        picked = [jnp.sum(jnp.where(which == pl.program_id(0) + h * blocks, steps, 0.0), axis=0, keepdims=True) for h in (0, 1)]
        return [v.astype(F32) * step for v, step in zip(high_low(q_ref[c]), picked)]

    for c in range(0, chips, 2):
        for h, (a, b) in enumerate(zip(values(c), values(c + 1))):
            at = c * half
            o_ref[0, 0, h, :, at:at+lanes] = jnp.where(lane < half, a, pltpu.roll(b, half, 1))
            o_ref[1, 0, h, :, at:at+lanes] = jnp.where(lane < half, pltpu.roll(a, half, 1), b)


def unpack(q, part, parts, before):
    chips, rows, lanes = q.shape
    rows -= 8
    wide = chips * lanes // 2
    blocks = rows // B
    args, specs = [q, q], [
        pl.BlockSpec((chips, B, lanes), lambda k: (0, k, 0)),
        pl.BlockSpec((chips, 8, lanes), lambda k: (0, rows // 8, 0)),
    ]
    if before is not None:
        args.append(before)
        specs.append(pl.BlockSpec(memory_space=pl.ANY))
    return pl.pallas_call(
        unpack_kernel,
        out_shape=jax.ShapeDtypeStruct((NPAR, parts, 2, rows, wide), F32),
        grid=(blocks,),
        in_specs=specs,
        out_specs=pl.BlockSpec((NPAR, 1, 2, B, wide), lambda k: (0, part, 0, k, 0)),
        input_output_aliases={} if before is None else {2: 0},
        compiler_params=pltpu.CompilerParams(vmem_limit_bytes=40*1024*1024),
        cost_estimate=pl.CostEstimate(flops=0, bytes_accessed=4*q.size+16*rows*wide, transcendentals=0),
    )(*args)


def unpack_plain(q):
    chips, rows, lanes = q.shape
    rows -= 8
    blocks = rows // B
    step = step_of(q[:, rows:rows+2*blocks]).reshape(chips, 2, blocks, 1, lanes)
    z = jnp.stack(high_low(q[:, :rows]), axis=1).astype(F32).reshape(chips, 2, blocks, B, lanes) * step
    z = z.reshape(chips, 2 * rows, NPAR, lanes // NPAR)
    return jnp.transpose(z, (2, 1, 0, 3)).reshape(NPAR, 2 * rows, chips * lanes // NPAR)


def take(x, axis, index):
    return lax.dynamic_index_in_dim(x, index, axis, keepdims=False)


def flip(x, bit, count):
    return lax.ppermute(x, "sub", [(i, i ^ bit) for i in range(count)])


def halve(x, axis, bit, me, count):
    own = jnp.where(me & bit, 1, 0)
    return take(x, axis, own) + flip(take(x, axis, 1 - own), bit, count)


def bit_orders(count):
    bits = [1 << i for i in range(count.bit_length() - 1)]
    plane = len(bits) // 2
    other = bits[:plane][::-1] + bits[plane:]
    return bits, other


def sum_shares(x, order, me, count, parent, partner):
    left = [1 << i for i in range(count.bit_length() - 1)][::-1]
    x = x.reshape((2,) * len(left) + (x.shape[0] // count, x.shape[1]))
    bit = order[0]
    axis = left.index(bit)
    own = jnp.where(me & bit, 1, 0)
    got = flip(take(x, axis, 1 - own), bit, count)
    kept = take(x, axis, own)
    left.remove(bit)
    x = jnp.stack([jnp.where(parent == p, kept, 0.0) + jnp.where(partner == p, got, 0.0) for p in range(NPAR)])
    for bit in order[1:]:
        x = halve(x, 1 + left.index(bit), bit, me, count)
        left.remove(bit)
    return x


def trade(mine, place):
    keep = take(mine, 0, place)
    got = lax.ppermute(take(mine, 0, 1 - place), "front", SWAP)
    return jnp.stack([jnp.where(place == 0, keep, got), jnp.where(place == 0, got, keep)])


def shards(count, piv_cols, trail_cols, row_end, parent_of):
    place = lax.axis_index("front")
    me = lax.axis_index("sub")
    tile_pivot = piv_cols.shape[2]
    n = NPAR * tile_pivot
    orders = bit_orders(count)
    other_piv = lax.ppermute(piv_cols[0, :LIVE], "front", SWAP)
    parent = parent_of[0]
    partners = [flip(parent_of, order[0], count)[0] for order in orders]
    info = jnp.concatenate([row_end[0], place[None].astype(jnp.int32)])
    packed, masked = pivot_gram(info, piv_cols, other_piv)
    trails = trail_gram(info, masked, trail_cols, PIECES)

    rows = packed.shape[0] // count
    packed = packed.reshape(count, rows, B)
    cut = rows // 16 * 8
    halves = (packed[:, :cut].reshape(-1, B), packed[:, cut:].reshape(-1, B))
    parts = [sum_shares(part, order, me, count, parent, partner) for part, order, partner in zip(halves, orders, partners)]
    gram = lax.all_gather(trade(jnp.concatenate(parts, axis=1), place), "sub", axis=0)

    shares = [sum_shares(t, orders[q % 2], me, count, parent, partners[q % 2]) for q, t in enumerate(trails)]
    share = jnp.concatenate(shares, axis=2)
    width = share.shape[1]
    trail = trade(share, place).reshape(NPAR * width, n)

    def gather(codes):
        theirs = lax.ppermute(codes, "front", SWAP)
        words = jnp.where(
            place == 0,
            jnp.concatenate([codes[:, :width], theirs[:, :width]], axis=1),
            jnp.concatenate([theirs[:, width:], codes[:, width:]], axis=1),
        )
        return lax.all_gather(words, "sub", axis=0)

    def own_columns(factor):
        return trade(jnp.stack([factor[:, :tile_pivot], factor[:, tile_pivot:]]), place)

    nb = n // B
    upper, codes, rest = chol_rows(0, nb // 2, n, NPAR * width, gram, trail)
    first = gather(codes)
    lower, codes = chol_rows(nb // 2, nb, n, NPAR * width, rest)
    second = gather(codes)
    if 2 * width == B:
        r_trail = unpack(second, 1, 2, unpack(first, 0, 2, None)).reshape(NPAR, n, -1)
    else:
        r_trail = jnp.concatenate([unpack_plain(first), unpack_plain(second)], axis=1)
    r_pivot = jnp.concatenate([own_columns(upper), own_columns(lower)], axis=1)
    return (r_pivot, r_trail)


def solution(mesh):
    count = mesh.shape["sub"]
    return jax.shard_map(
        lambda *args: shards(count, *args),
        mesh=mesh,
        in_specs=(P("sub", None, "front"), P("sub", None, "front"), P("sub", None), P("sub")),
        out_specs=(P(None, None, "front"), P(None, None, "front")),
        check_vma=False,
    )
```

```python
import jax, jax.numpy as jnp
from jax import lax
from jax.experimental import pallas as pl
from jax.experimental.pallas import tpu as pltpu
from jax.sharding import PartitionSpec as P
B=128
F32=jnp.float32
BF=jnp.bfloat16
LIVE = 1280
NPAR = 2
ZS = 4
LEVELS = 32766.0
SWAP = [(0, 1), (1, 0)]

def split(x):
    hi = x.astype(BF)
    return hi, (x - hi.astype(F32)).astype(BF)

def factor_block(d_ref, w_ref, fillers):
    rows8 = (8, B)
    for g in range(B // 8):
        xs, xi = [], []
        for i in range(8):
            row = d_ref[8*g+i:8*g+i+1, :]
            xs.append(jnp.broadcast_to(row[:, :B], rows8))
            xi.append(jnp.broadcast_to(row[:, B:], rows8))
        s = {}
        for i in range(8):
            for j in range(i, 8):
                s[i, j] = jnp.broadcast_to(xs[i][:, 8*g+j:8*g+j+1], rows8)
        for i in range(8):
            rs = lax.rsqrt(s[i, i])
            inv = rs * rs
            w_ref[8*g+i:8*g+i+1, :B] = (xs[i] * rs)[:1]
            w_ref[8*g+i:8*g+i+1, B:] = (xi[i] * rs)[:1]
            for r in range(8):
                if r == i: continue
                m = (s[r, i] if r < i else s[i, r]) * inv
                for j in range(max(r, i+1), 8):
                    s[r, j] = s[r, j] - m * s[i, j]
                xs[r] = xs[r] - m * xs[i]
                xi[r] = xi[r] - m * xi[i]
            s[i, i] = inv
        ys = [xs[i] * s[i, i] for i in range(8)]
        yi = [xi[i] * s[i, i] for i in range(8)]
        for r in range(g+1, B // 8):
            blk = d_ref[8*r:8*r+8, :B]
            bi = d_ref[8*r:8*r+8, B:]
            cols = [jnp.broadcast_to(blk[:, 8*g+i:8*g+i+1], rows8) for i in range(8)]
            for i in range(8):
                blk = blk - cols[i] * ys[i]
                bi = bi - cols[i] * yi[i]
            d_ref[8*r:8*r+8, :B] = blk
            d_ref[8*r:8*r+8, B:] = bi
        if fillers:
            fillers.pop(0)()
    while fillers:
        fillers.pop(0)()


def gram_rows(i, j):
    t = j // 2
    return j % 2, (t * t + t + i) * B


def chol_kernel(first, last, *refs):
    begin = first == 0
    if begin:
        info_ref, *refs = refs
        place, myz, myq = here(info_ref)
        planes = len(refs) - 12
        slots, (keep_ref, got_ref), refs = refs[:planes], refs[planes:planes+2], refs[planes+2:]
    else:
        in_ref, *refs = refs
    r_ref, q_ref, *refs = refs
    if begin:
        out_ref, g_ref, t_ref, *refs = refs
        share = g_ref.shape[2]
        for q, slot in enumerate(slots):
            for r in range(slot.shape[0]):
                chip = (myz ^ r) * planes + (myq ^ q)
                for c in range(2):
                    g_ref[chip, place ^ c] = slot[r, c*share:(c+1)*share, :]
        wide = keep_ref.shape[0]
        t_ref[pl.ds(pl.multiple_of(place * wide, wide), wide), :] = keep_ref[...]
        t_ref[pl.ds(pl.multiple_of((1 - place) * wide, wide), wide), :] = got_ref[...]
    s_ref, z_ref, d_ref, w_ref, rhs_ref = refs
    nt = z_ref.shape[1]
    n = r_ref.shape[1]
    nb = n // B
    base = first * B
    ri = lax.broadcasted_iota(jnp.int32, (B, B), 0)
    ci = lax.broadcasted_iota(jnp.int32, (B, B), 1)

    def gram_parts(i, j):
        core, at = gram_rows(i, j)
        share = g_ref.shape[2]
        end, row = at + B, 0
        while at < end:
            chip, off = at // share, at % share
            size = min(share - off, end - at)
            yield row, g_ref[chip, core, off:off+size, :]
            at, row = at + size, row + size

    def load(k, lo, hi):
        if not begin:
            return in_ref[(k-first)*B:(k-first+1)*B, lo-base:hi-base]
        for j in range(lo // B, min(hi, n) // B):
            for row, part in gram_parts(k, j):
                s_ref[k*B+row:k*B+row+part.shape[0], j*B:(j+1)*B] = part
        if hi > n:
            s_ref[k*B:(k+1)*B, n:] = jnp.transpose(t_ref[:, k*B:(k+1)*B])
        return s_ref[k*B:(k+1)*B, lo:hi]

    def current(k, lo, hi):
        return load(k, lo, hi) if k == first else s_ref[k*B-base:(k+1)*B-base, lo-base:hi-base]

    def update(k, i):
        def run():
            lo = i * B
            lhs = split(jnp.transpose(r_ref[k*B-base:(k+1)*B-base, lo:lo+B]))
            lhs = jnp.concatenate([lhs[0], lhs[0], lhs[1]], axis=1)
            upd = jnp.dot(lhs, rhs_ref[k % 2, :, lo-base:], preferred_element_type=F32)
            if i >= last and k == last - 1:
                out_ref[(i-last)*B:(i-last+1)*B, lo-last*B:] = s_ref[lo-base:lo-base+B, lo-base:] - upd
            elif k > first:
                s_ref[lo-base:lo-base+B, lo-base:] = s_ref[lo-base:lo-base+B, lo-base:] - upd
            elif begin:
                for j in range(i, nb):
                    for row, part in gram_parts(i, j):
                        size = part.shape[0]
                        s_ref[lo+row:lo+row+size, j*B:(j+1)*B] = part - upd[row:row+size, (j-i)*B:(j-i+1)*B]
                s_ref[lo:lo+B, n:] = jnp.transpose(t_ref[:, lo:lo+B]) - upd[:, n-lo:]
            else:
                s_ref[lo-base:lo-base+B, lo-base:] = in_ref[lo-base:lo-base+B, lo-base:] - upd
        return run

    fillers = []
    for k in range(first, last):
        lo = k * B
        at = lo - base
        d_ref[:, :B] = current(k, lo, lo + B)
        d_ref[:, B:] = jnp.where(ri == ci, 1.0, 0.0).astype(F32)
        factor_block(d_ref, w_ref, fillers)
        fillers = []
        if k:
            r_ref[at:at+B, :lo] = jnp.zeros((B, lo), F32)
        r_ref[at:at+B, lo:lo+B] = jnp.where(ci >= ri, w_ref[:, :B], 0.0)
        wh, wl = split(w_ref[:, B:])
        w3 = jnp.concatenate([wh, wh, wl], axis=1)
        rh, rl = split(current(k, lo + B, n + nt))
        p = jnp.dot(w3, jnp.concatenate([rh, rl, rh], axis=0), preferred_element_type=F32)
        if k < nb - 1:
            r_ref[at:at+B, lo+B:] = p[:, :n-lo-B]
        z_ref[at:at+B, :] = p[:, n-lo-B:]
        ph, pll = split(p)
        rhs_ref[k % 2, 0:B, lo+B-base:] = ph
        rhs_ref[k % 2, B:2*B, lo+B-base:] = pll
        rhs_ref[k % 2, 2*B:, lo+B-base:] = ph
        if k < nb - 1:
            update(k, k+1)()
            fillers = [update(k, i) for i in range(k+2, nb)]
    for fill in fillers:
        fill()
    count = last - first
    coded = [encode(z_ref[k*B:(k+1)*B, :]) for k in range(count)]
    for k in range(count // 2):
        q_ref[k*B:(k+1)*B, :] = join(coded[k][0], coded[k + count // 2][0])
    scales = [join(e, mant) for _, e, mant in coded]
    scales += [jnp.zeros_like(scales[0])] * (8 - count)
    q_ref[count//2*B:, :] = jnp.concatenate(scales, axis=0)


def here(info_ref):
    end = info_ref.shape[0]
    return info_ref[end - 3], info_ref[end - 2], info_ref[end - 1]


def scale_of(e, mant):
    return mant.astype(F32) * jnp.exp2(e.astype(F32)) * (1.0 / (16384.0 * LEVELS))


def encode(x):
    top = jnp.maximum(jnp.max(jnp.abs(x), axis=0, keepdims=True), 1e-30)
    e = jnp.ceil(jnp.log2(top)).astype(jnp.int32)
    mant = jnp.minimum(jnp.ceil(top * jnp.exp2(-e.astype(F32)) * 16384.0) + 1.0, 32767.0).astype(jnp.int32)
    codes = jnp.clip(jnp.round(x * (1.0 / scale_of(e, mant))), -LEVELS, LEVELS)
    return codes.astype(jnp.int32), e, mant


def join(high, low):
    return jnp.bitwise_or(jnp.left_shift(high, 16), jnp.bitwise_and(low, 65535))


def high_low(word):
    return jnp.right_shift(word, 16), jnp.right_shift(jnp.left_shift(word, 16), 16)


def call(kernel, info, args, outs, scratch=(), blocks=None, cost=0, limit=24):
    blocks = blocks or [arg.shape for arg in args]
    return pl.pallas_call(
        kernel,
        out_shape=tuple(outs),
        grid_spec=pltpu.PrefetchScalarGridSpec(
            num_scalar_prefetch=1,
            grid=(1,),
            in_specs=[pl.BlockSpec(block, lambda i, info, zeros=(0,) * len(block): zeros) for block in blocks],
            out_specs=tuple(pl.BlockSpec(out.shape, lambda i, info, zeros=(0,) * len(out.shape): zeros) for out in outs),
            scratch_shapes=list(scratch),
        ),
        compiler_params=pltpu.CompilerParams(vmem_limit_bytes=limit*1024*1024),
        cost_estimate=pl.CostEstimate(flops=cost, bytes_accessed=4*1024*1024, transcendentals=0),
    )(info, *args)


def real(*shape):
    return jax.ShapeDtypeStruct(shape, F32)


def short(*shape):
    return jax.ShapeDtypeStruct(shape, jnp.int16)


def chol_rows(first, last, n, nt, *args):
    vmem = pl.BlockSpec(memory_space=pltpu.VMEM)
    rows = (last - first) * B
    wide = n + nt - first * B
    outs = [real(rows, n), jax.ShapeDtypeStruct((rows // 2 + 8, nt), jnp.int32)]
    scratch = [
        pltpu.VMEM((n - first * B, wide), F32),
        pltpu.VMEM((rows, nt), F32),
        pltpu.VMEM((B, 2*B), F32),
        pltpu.VMEM((B, 2*B), F32),
        pltpu.VMEM((2, 3*B, wide), BF),
    ]
    specs = [vmem] * len(args)
    if first == 0:
        outs.append(real(n - last * B, n + nt - last * B))
        planes = len(args) - 3
        zs, share = args[1].shape[0], args[1].shape[1] // 2
        scratch = [pltpu.VMEM((planes * zs, 2, share, B), F32), pltpu.VMEM((nt, n), F32)] + scratch
        specs[0] = pl.BlockSpec(memory_space=pltpu.SMEM)
    return pl.pallas_call(
        lambda *refs: chol_kernel(first, last, *refs),
        out_shape=tuple(outs),
        in_specs=specs,
        out_specs=(vmem,) * len(outs),
        scratch_shapes=scratch,
        compiler_params=pltpu.CompilerParams(vmem_limit_bytes=32*1024*1024),
        cost_estimate=pl.CostEstimate(flops=30*n*n*n // 2, bytes_accessed=4*rows*n, transcendentals=0),
    )(*args)


DIMS = (((0,), (0,)), ((), ()))


def pivot_kernel(info_ref, own_ref, other_ref, a_ref, *refs):
    slots, g_ref = refs[:-1], refs[-1]
    live, tile = other_ref.shape
    n = a_ref.shape[1]
    place, myz, myq = here(info_ref)
    rows = lax.broadcasted_iota(jnp.int32, (live, B), 0)
    zero = jnp.zeros((live, B), BF)
    per = tile // B
    for half, ref in ((place, own_ref.at[0]), (1 - place, other_ref)):
        for j in range(per):
            end = info_ref[half * per + j]
            at = pl.multiple_of(half * tile + j * B, B)
            a_ref[:, pl.ds(at, B)] = jnp.where(rows < end, ref[:, j*B:(j+1)*B], zero)
    for t in range(n // B // 2):
        at = pl.multiple_of((2 * t + place) * B, B)
        out = lax.dot_general(a_ref[:, :(2*t+2)*B], a_ref[:, pl.ds(at, B)], DIMS, preferred_element_type=F32)
        g_ref[(t*t+t)*B:(t*t+3*t+2)*B, :] = out
    share = slots[0].shape[0] // ZS
    for q, slot in enumerate(slots):
        for z in range(ZS):
            at = pl.multiple_of((z * len(slots) + (myq ^ q)) * share, 8)
            slot[z*share:(z+1)*share, :] = g_ref[pl.ds(at, share), :]
        if q:
            slot[ZS*share:, :] = jnp.full((8, B), info_ref[info_ref.shape[0] - 4], jnp.int32).astype(F32)


def pivot_plane_kernel(info_ref, own_ref, *refs):
    got, slots = refs[:-ZS], refs[-ZS:]
    share = own_ref.shape[0] // ZS
    place, myz, myq = here(info_ref)
    parent = info_ref[info_ref.shape[0] - 4]
    theirs = [jnp.broadcast_to(ref[ZS*share:ZS*share+1, :], (share, B)) for ref in got]
    for r, slot in enumerate(slots):
        at = pl.multiple_of((myz ^ r) * share, 8)
        own = own_ref[pl.ds(at, share), :]
        parts = [ref[pl.ds(at, share), :] for ref in got]
        for p in range(NPAR):
            total = jnp.where(parent == p, own, 0.0)
            for part, their in zip(parts, theirs):
                total = total + jnp.where(their == p, part, 0.0)
            slot[p*share:(p+1)*share, :] = total


def pivot_line_kernel(info_ref, own_ref, *refs):
    got, outs = refs[:-2], refs[-2:]
    share = own_ref.shape[0] // NPAR
    place, myz, myq = here(info_ref)
    for out, p in zip(outs, (place, 1 - place)):
        at = pl.ds(pl.multiple_of(p * share, 8), share)
        total = own_ref[at, :]
        for ref in got:
            total = total + ref[at, :]
        out[...] = total


def trail_kernel(info_ref, a_ref, trail_ref, *refs):
    slots, t_ref = refs[:-1], refs[-1]
    live, n = a_ref.shape
    place, myz, myq = here(info_ref)
    rows = lax.broadcasted_iota(jnp.int32, (live, B), 0)
    zero = jnp.zeros((live, B), BF)
    per = trail_ref.shape[2] // B
    group = per // ZS
    width = slots[0].shape[0] // ZS
    scales = [[] for _ in slots]
    for z in range(ZS):
        cols = []
        for h in range(z * group, (z + 1) * group):
            end = info_ref[n // B + place * per + h]
            cols.append(jnp.where(rows < end, trail_ref[0, :, h*B:(h+1)*B], zero))
        t_ref[z % 2] = lax.dot_general(jnp.concatenate(cols, axis=1), a_ref[...], DIMS, preferred_element_type=F32)
        for q, slot in enumerate(slots):
            at = pl.multiple_of((myq ^ q) * width, width)
            part = t_ref[z % 2, pl.ds(at, width), :]
            if q:
                part, e, mant = encode(part)
                scales[q].append((e, mant))
            slot[z*width:(z+1)*width, :] = part.astype(slot.dtype)
    for q, slot in enumerate(slots):
        if q:
            spare = [jnp.full((1, n), info_ref[info_ref.shape[0] - 4], jnp.int32)]
            write_scales(slot, ZS * width, [e for e, _ in scales[q]] + [m for _, m in scales[q]] + spare)


def write_scales(slot, at, rows):
    rows = rows + [jnp.zeros_like(rows[0])] * (16 - len(rows))
    slot[at:at+16, :] = jnp.concatenate(rows, axis=0).astype(jnp.int16)


def row_of(tile, index):
    rows = lax.broadcasted_iota(jnp.int32, tile.shape, 0)
    return jnp.sum(jnp.where(rows == index, tile, 0), axis=0, keepdims=True)


def trail_plane_kernel(info_ref, own_ref, *refs):
    got, slots = refs[:-ZS], refs[-ZS:]
    width = own_ref.shape[0] // ZS
    place, myz, myq = here(info_ref)
    parent = info_ref[info_ref.shape[0] - 4]
    tiles = [ref[ZS*width:, :].astype(jnp.int32) for ref in got]
    for r, slot in enumerate(slots):
        z = myz ^ r
        at = pl.multiple_of(z * width, width)
        own = own_ref[pl.ds(at, width), :]
        parts = [ref[pl.ds(at, width), :].astype(jnp.int32).astype(F32) for ref in got]
        steps = [scale_of(row_of(tile, z), row_of(tile, ZS + z)) for tile in tiles]
        scales = []
        for p in range(NPAR):
            total = jnp.where(parent == p, own, 0.0)
            for part, step, tile in zip(parts, steps, tiles):
                total = total + part * jnp.where(tile[2*ZS:2*ZS+1, :] == p, step, 0.0)
            if r:
                total, e, mant = encode(total)
                scales.append((e, mant))
            slot[p*width:(p+1)*width, :] = total.astype(slot.dtype)
        if r:
            write_scales(slot, NPAR * width, [e for e, _ in scales] + [m for _, m in scales])


def trail_line_kernel(info_ref, own_ref, *refs):
    got, outs = refs[:-2], refs[-2:]
    width = own_ref.shape[0] // NPAR
    place, myz, myq = here(info_ref)
    tiles = [ref[NPAR*width:, :].astype(jnp.int32) for ref in got]
    for out, p in zip(outs, (place, 1 - place)):
        at = pl.ds(pl.multiple_of(p * width, width), width)
        total = own_ref[at, :]
        for ref, tile in zip(got, tiles):
            total = total + ref[at, :].astype(jnp.int32).astype(F32) * scale_of(row_of(tile, p), row_of(tile, NPAR + p))
        out[...] = total


def unpack_kernel(info_ref, *refs):
    o_ref = refs[-1]
    planes = 4
    words, scales = refs[:planes], refs[planes:2*planes]
    place, myz, myq = here(info_ref)
    zs, rows, lanes = words[0].shape
    half = lanes // 2
    lane = lax.broadcasted_iota(jnp.int32, (rows, lanes), 1)
    which = lax.broadcasted_iota(jnp.int32, (8, lanes), 0)
    blocks = pl.num_programs(0)
    odd = (myq & 1) == 1

    def values(q, r):
        steps = scale_of(*high_low(scales[q][r]))
        picked = [jnp.sum(jnp.where(which == pl.program_id(0) + h * blocks, steps, 0.0), axis=0, keepdims=True) for h in (0, 1)]
        return [v.astype(F32) * step for v, step in zip(high_low(words[q][r]), picked)]

    for q in range(0, planes, 2):
        for r in range(zs):
            at = pl.multiple_of(((myz ^ r) * planes + ((myq ^ q) & 2)) * half, lanes)
            for h, (a, b) in enumerate(zip(values(q, r), values(q + 1, r))):
                a, b = jnp.where(odd, b, a), jnp.where(odd, a, b)
                o_ref[0, 0, h, :, pl.ds(at, lanes)] = jnp.where(lane < half, a, pltpu.roll(b, half, 1))
                o_ref[1, 0, h, :, pl.ds(at, lanes)] = jnp.where(lane < half, pltpu.roll(a, half, 1), b)


def unpack(info, slots, part, parts, before):
    zs, rows, lanes = slots[0].shape
    rows -= 8
    wide = zs * len(slots) * lanes // 2
    blocks = rows // B
    args = list(slots) * 2
    specs = [pl.BlockSpec((zs, B, lanes), lambda k, info: (0, k, 0))] * len(slots)
    specs += [pl.BlockSpec((zs, 8, lanes), lambda k, info: (0, rows // 8, 0))] * len(slots)
    if before is not None:
        args.append(before)
        specs.append(pl.BlockSpec(memory_space=pl.ANY))
    return pl.pallas_call(
        unpack_kernel,
        out_shape=real(NPAR, parts, 2, rows, wide),
        grid_spec=pltpu.PrefetchScalarGridSpec(
            num_scalar_prefetch=1,
            grid=(blocks,),
            in_specs=specs,
            out_specs=pl.BlockSpec((NPAR, 1, 2, B, wide), lambda k, info: (0, part, 0, k, 0)),
        ),
        input_output_aliases={} if before is None else {len(args): 0},
        compiler_params=pltpu.CompilerParams(vmem_limit_bytes=32*1024*1024),
        cost_estimate=pl.CostEstimate(flops=0, bytes_accessed=20*rows*wide, transcendentals=0),
    )(info, *args)


def unpack_plain(q):
    chips, rows, lanes = q.shape
    rows -= 8
    blocks = rows // B
    step = scale_of(*high_low(q[:, rows:rows+2*blocks])).reshape(chips, 2, blocks, 1, lanes)
    z = jnp.stack(high_low(q[:, :rows]), axis=1).astype(F32).reshape(chips, 2, blocks, B, lanes) * step
    z = z.reshape(chips, 2 * rows, NPAR, lanes // NPAR)
    return jnp.transpose(z, (2, 1, 0, 3)).reshape(NPAR, 2 * rows, chips * lanes // NPAR)


def take(x, axis, index):
    return lax.dynamic_index_in_dim(x, index, axis, keepdims=False)


def trade(mine, place):
    keep = take(mine, 0, place)
    got = lax.ppermute(take(mine, 0, 1 - place), "front", SWAP)
    return jnp.stack([jnp.where(place == 0, keep, got), jnp.where(place == 0, got, keep)])


def shards(count, piv_cols, trail_cols, row_end, parent_of):
    place = lax.axis_index("front")
    me = lax.axis_index("sub")
    planes = count // ZS
    myz, myq = me // planes, me % planes
    tile_pivot, tile_trail = piv_cols.shape[2], trail_cols.shape[2]
    n = NPAR * tile_pivot
    width = tile_trail // count
    blocks = n // B // 2
    share = (blocks * blocks + blocks) * B // count

    def flip(x, mask):
        return lax.ppermute(x, "sub", [(i, i ^ mask) for i in range(count)])

    def over_plane(slots):
        return [flip(x, q) for q, x in enumerate(slots) if q]

    def over_line(slots):
        return [flip(x, r * planes) for r, x in enumerate(slots) if r]

    def everywhere(x):
        line = jnp.stack([x] + over_line([x] * ZS))
        return [line] + over_plane([line] * planes)

    other_piv = lax.ppermute(piv_cols[0, :LIVE], "front", SWAP)
    info = jnp.concatenate([row_end[0], parent_of, jnp.stack([place, myz, myq]).astype(jnp.int32)])

    outs = [jax.ShapeDtypeStruct((LIVE, n), BF), real(ZS * share, B)] + [real(ZS * share + 8, B)] * (planes - 1)
    masked, *slots = call(
        pivot_kernel, info, (piv_cols, other_piv), outs, [pltpu.VMEM((count * share, B), F32)],
        blocks=[(1, LIVE, tile_pivot), (LIVE, tile_pivot)], cost=LIVE*n*n,
    )
    got = over_plane(slots)
    outs = [real(ZS * width, n)] + [short(ZS * width + 16, n)] * (planes - 1)
    trails = call(
        trail_kernel, info, (masked, trail_cols), outs, [pltpu.VMEM((2, planes * width, n), F32)],
        blocks=[(LIVE, n), (1, LIVE, tile_trail)], cost=2*LIVE*n*tile_trail, limit=32,
    )
    got_trails = over_plane(trails)

    slots = call(pivot_plane_kernel, info, (slots[0], *got), [real(NPAR * share, B)] * ZS)
    keep, give = call(pivot_line_kernel, info, (slots[0], *over_line(slots)), [real(share, B)] * 2)
    grams = everywhere(jnp.concatenate([keep, lax.ppermute(give, "front", SWAP)], axis=0))

    outs = [real(NPAR * width, n)] + [short(NPAR * width + 16, n)] * (ZS - 1)
    trails = call(trail_plane_kernel, info, (trails[0], *got_trails), outs)
    keep, give = call(trail_line_kernel, info, (trails[0], *over_line(trails)), [real(width, n)] * 2)
    got = lax.ppermute(give, "front", SWAP)

    def gather(codes):
        theirs = lax.ppermute(codes, "front", SWAP)
        words = jnp.where(
            place == 0,
            jnp.concatenate([codes[:, :width], theirs[:, :width]], axis=1),
            jnp.concatenate([theirs[:, width:], codes[:, width:]], axis=1),
        )
        return everywhere(words)

    def own_columns(factor):
        return trade(jnp.stack([factor[:, :tile_pivot], factor[:, tile_pivot:]]), place)

    def in_order(slots):
        every = jnp.stack(slots)
        every = jnp.take(jnp.take(every, jnp.arange(planes) ^ myq, axis=0), jnp.arange(ZS) ^ myz, axis=1)
        return jnp.swapaxes(every, 0, 1).reshape((count,) + every.shape[2:])

    nb = n // B
    upper, codes, rest = chol_rows(0, nb // 2, n, NPAR * width, info, *grams, keep, got)
    first = gather(codes)
    lower, codes = chol_rows(nb // 2, nb, n, NPAR * width, rest)
    second = gather(codes)
    if 2 * width == B and planes == 4:
        r_trail = unpack(info, second, 1, 2, unpack(info, first, 0, 2, None)).reshape(NPAR, n, -1)
    else:
        r_trail = jnp.concatenate([unpack_plain(in_order(first)), unpack_plain(in_order(second))], axis=1)
    r_pivot = jnp.concatenate([own_columns(upper), own_columns(lower)], axis=1)
    return (r_pivot, r_trail)


def solution(mesh):
    count = mesh.shape["sub"]
    return jax.shard_map(
        lambda *args: shards(count, *args),
        mesh=mesh,
        in_specs=(P("sub", None, "front"), P("sub", None, "front"), P("sub", None), P("sub")),
        out_specs=(P(None, None, "front"), P(None, None, "front")),
        check_vma=False,
    )
```

```python
import jax, jax.numpy as jnp
from jax import lax
from jax.experimental import pallas as pl
from jax.experimental.pallas import tpu as pltpu
from jax.sharding import PartitionSpec as P
B=128
F32=jnp.float32
BF=jnp.bfloat16
LIVE = 1280
NPAR = 2
ZS = 4
LEVELS = 32766.0
SWAP = [(0, 1), (1, 0)]

def split(x):
    hi = x.astype(BF)
    return hi, (x - hi.astype(F32)).astype(BF)

def factor_block(d_ref, w_ref, fillers):
    rows8 = (8, B)
    for g in range(B // 8):
        xs, xi = [], []
        for i in range(8):
            row = d_ref[8*g+i:8*g+i+1, :]
            xs.append(jnp.broadcast_to(row[:, :B], rows8))
            xi.append(jnp.broadcast_to(row[:, B:], rows8))
        s = {}
        for i in range(8):
            for j in range(i, 8):
                s[i, j] = jnp.broadcast_to(xs[i][:, 8*g+j:8*g+j+1], rows8)
        after = 8 * (g + 1)
        if after < B:
            blk = d_ref[after:after+8, :B]
            bi = d_ref[after:after+8, B:]
            cols = [jnp.broadcast_to(blk[:, 8*g+i:8*g+i+1], rows8) for i in range(8)]
        for i in range(8):
            rs = lax.rsqrt(s[i, i])
            inv = rs * rs
            w_ref[8*g+i:8*g+i+1, :B] = (xs[i] * rs)[:1]
            w_ref[8*g+i:8*g+i+1, B:] = (xi[i] * rs)[:1]
            for r in range(8):
                if r == i: continue
                m = (s[r, i] if r < i else s[i, r]) * inv
                for j in range(max(r, i+1), 8):
                    s[r, j] = s[r, j] - m * s[i, j]
                xs[r] = xs[r] - m * xs[i]
                xi[r] = xi[r] - m * xi[i]
            s[i, i] = inv
            if after < B:
                m = cols[i] * inv
                blk = blk - m * xs[i]
                bi = bi - m * xi[i]
                for j in range(i+1, 8):
                    cols[j] = cols[j] - m * s[i, j]
        if after < B:
            d_ref[after:after+8, :B] = blk
            d_ref[after:after+8, B:] = bi
        ys = [xs[i] * s[i, i] for i in range(8)]
        yi = [xi[i] * s[i, i] for i in range(8)]
        for r in range(g+2, B // 8):
            blk = d_ref[8*r:8*r+8, :B]
            bi = d_ref[8*r:8*r+8, B:]
            cols = [jnp.broadcast_to(blk[:, 8*g+i:8*g+i+1], rows8) for i in range(8)]
            for i in range(8):
                blk = blk - cols[i] * ys[i]
                bi = bi - cols[i] * yi[i]
            d_ref[8*r:8*r+8, :B] = blk
            d_ref[8*r:8*r+8, B:] = bi
        if fillers:
            fillers.pop(0)()
    while fillers:
        fillers.pop(0)()


def gram_rows(i, j, nb):
    t = j // 2
    if j == nb - 1:
        return (0, (t * t + 2 * t + 1 + i) * B) if i < 2 else (1, (t * t + t + i - 2) * B)
    return j % 2, (t * t + (j % 2) * t + i) * B


def chol_kernel(first, last, n, planes, spots, *refs):
    begin = first == 0
    info_ref, *refs = refs
    place, myz, myq = here(info_ref)
    if begin:
        slots, (keep_ref, got_ref), refs = refs[:len(spots)], refs[len(spots):len(spots)+2], refs[len(spots)+2:]
    else:
        in_ref, _, *refs = refs
    r_keep_ref, r_give_ref, q_ref, *refs = refs
    if begin:
        out_ref, g_ref, t_ref, *refs = refs
        share = g_ref.shape[2]
        for slot, (q, start) in zip(slots, spots):
            for r in range(slot.shape[0]):
                chip = (myz ^ (start + r)) * planes + (myq ^ q)
                for c in range(2):
                    g_ref[chip, place ^ c] = slot[r, c*share:(c+1)*share, :]
        wide = keep_ref.shape[0]
        t_ref[pl.ds(pl.multiple_of(place * wide, wide), wide), :] = keep_ref[...]
        t_ref[pl.ds(pl.multiple_of((1 - place) * wide, wide), wide), :] = got_ref[...]
    r_ref, s_ref, z_ref, d_ref, w_ref, rhs_ref = refs
    nt = z_ref.shape[1]
    nb = n // B
    base = first * B
    ri = lax.broadcasted_iota(jnp.int32, (B, B), 0)
    ci = lax.broadcasted_iota(jnp.int32, (B, B), 1)

    def gram_parts(i, j):
        core, at = gram_rows(i, j, nb)
        share = g_ref.shape[2]
        end, row = at + B, 0
        while at < end:
            chip, off = at // share, at % share
            size = min(share - off, end - at)
            yield row, g_ref[chip, core, off:off+size, :]
            at, row = at + size, row + size

    def load(k, lo, hi):
        if not begin:
            return in_ref[(k-first)*B:(k-first+1)*B, lo-base:hi-base]
        for j in range(lo // B, min(hi, n) // B):
            for row, part in gram_parts(k, j):
                s_ref[k*B+row:k*B+row+part.shape[0], j*B:(j+1)*B] = part
        if hi > n:
            s_ref[k*B:(k+1)*B, n:] = jnp.transpose(t_ref[:, k*B:(k+1)*B])
        return s_ref[k*B:(k+1)*B, lo:hi]

    def current(k, lo, hi):
        return load(k, lo, hi) if k == first else s_ref[k*B-base:(k+1)*B-base, lo-base:hi-base]

    def update(k, i):
        def run():
            lo = i * B
            lhs = split(jnp.transpose(r_ref[k*B-base:(k+1)*B-base, lo:lo+B]))
            lhs = jnp.concatenate([lhs[0], lhs[0], lhs[1]], axis=1)
            upd = jnp.dot(lhs, rhs_ref[k % 2, :, lo-base:], preferred_element_type=F32)
            if i >= last and k == last - 1:
                out_ref[(i-last)*B:(i-last+1)*B, lo-last*B:] = s_ref[lo-base:lo-base+B, lo-base:] - upd
            elif k > first:
                s_ref[lo-base:lo-base+B, lo-base:] = s_ref[lo-base:lo-base+B, lo-base:] - upd
            elif begin:
                for j in range(i, nb):
                    for row, part in gram_parts(i, j):
                        size = part.shape[0]
                        s_ref[lo+row:lo+row+size, j*B:(j+1)*B] = part - upd[row:row+size, (j-i)*B:(j-i+1)*B]
                s_ref[lo:lo+B, n:] = jnp.transpose(t_ref[:, lo:lo+B]) - upd[:, n-lo:]
            else:
                s_ref[lo-base:lo-base+B, lo-base:] = in_ref[lo-base:lo-base+B, lo-base:] - upd
        return run

    fillers = []
    for k in range(first, last):
        lo = k * B
        at = lo - base
        d_ref[:, :B] = current(k, lo, lo + B)
        d_ref[:, B:] = jnp.where(ri == ci, 1.0, 0.0).astype(F32)
        factor_block(d_ref, w_ref, fillers)
        fillers = []
        if k:
            r_ref[at:at+B, :lo] = jnp.zeros((B, lo), F32)
        r_ref[at:at+B, lo:lo+B] = jnp.where(ci >= ri, w_ref[:, :B], 0.0)
        wh, wl = split(w_ref[:, B:])
        w3 = jnp.concatenate([wh, wh, wl], axis=1)
        rh, rl = split(current(k, lo + B, n + nt))
        p = jnp.dot(w3, jnp.concatenate([rh, rl, rh], axis=0), preferred_element_type=F32)
        if k < nb - 1:
            r_ref[at:at+B, lo+B:] = p[:, :n-lo-B]
        z_ref[at:at+B, :] = p[:, n-lo-B:]
        ph, pll = split(p)
        rhs_ref[k % 2, 0:B, lo+B-base:] = ph
        rhs_ref[k % 2, B:2*B, lo+B-base:] = pll
        rhs_ref[k % 2, 2*B:, lo+B-base:] = ph
        if k < nb - 1:
            update(k, k+1)()
            fillers = [update(k, i) for i in range(k+2, nb)]
    for fill in fillers:
        fill()
    tile = r_keep_ref.shape[1]
    r_keep_ref[...] = r_ref[:, pl.ds(pl.multiple_of(place * tile, B), tile)]
    r_give_ref[...] = r_ref[:, pl.ds(pl.multiple_of((1 - place) * tile, B), tile)]
    count = last - first
    coded = [encode(z_ref[k*B:(k+1)*B, :]) for k in range(count)]
    for k in range(count // 2):
        q_ref[k*B:(k+1)*B, :] = join(coded[k][0], coded[k + count // 2][0])
    scales = [join(e, mant) for _, e, mant in coded]
    scales += [jnp.zeros_like(scales[0])] * (8 - count)
    q_ref[count//2*B:, :] = jnp.concatenate(scales, axis=0)


def here(info_ref):
    end = info_ref.shape[0]
    return info_ref[end - 3], info_ref[end - 2], info_ref[end - 1]


def scale_of(e, mant):
    return mant.astype(F32) * jnp.exp2(e.astype(F32)) * (1.0 / (16384.0 * LEVELS))


def encode(x):
    top = jnp.maximum(jnp.max(jnp.abs(x), axis=0, keepdims=True), 1e-30)
    e = jnp.ceil(jnp.log2(top)).astype(jnp.int32)
    mant = jnp.minimum(jnp.ceil(top * jnp.exp2(-e.astype(F32)) * 16384.0) + 1.0, 32767.0).astype(jnp.int32)
    codes = jnp.clip(jnp.round(x * (1.0 / scale_of(e, mant))), -LEVELS, LEVELS)
    return codes.astype(jnp.int32), e, mant


def join(high, low):
    return jnp.bitwise_or(jnp.left_shift(high, 16), jnp.bitwise_and(low, 65535))


def high_low(word):
    return jnp.right_shift(word, 16), jnp.right_shift(jnp.left_shift(word, 16), 16)


def call(kernel, info, args, outs, scratch=(), far=(), cost=0, limit=24):
    hbm = pl.BlockSpec(memory_space=pltpu.HBM)
    return pl.pallas_call(
        kernel,
        out_shape=tuple(outs),
        grid_spec=pltpu.PrefetchScalarGridSpec(
            num_scalar_prefetch=1,
            grid=(1,),
            in_specs=[
                hbm if at in far else pl.BlockSpec(arg.shape, lambda i, info, zeros=(0,) * len(arg.shape): zeros)
                for at, arg in enumerate(args)
            ],
            out_specs=tuple(pl.BlockSpec(out.shape, lambda i, info, zeros=(0,) * len(out.shape): zeros) for out in outs),
            scratch_shapes=list(scratch),
        ),
        compiler_params=pltpu.CompilerParams(vmem_limit_bytes=limit*1024*1024),
        cost_estimate=pl.CostEstimate(flops=cost, bytes_accessed=4*1024*1024, transcendentals=0),
    )(info, *args)


def real(*shape):
    return jax.ShapeDtypeStruct(shape, F32)


def short(*shape):
    return jax.ShapeDtypeStruct(shape, jnp.int16)


def chol_rows(first, last, n, nt, planes, spots, *args):
    vmem = pl.BlockSpec(memory_space=pltpu.VMEM)
    rows = (last - first) * B
    wide = n + nt - first * B
    outs = [real(rows, n // 2), real(rows, n // 2), jax.ShapeDtypeStruct((rows // 2 + 8, nt), jnp.int32)]
    scratch = [
        pltpu.VMEM((rows, n), F32),
        pltpu.VMEM((n - first * B, wide), F32),
        pltpu.VMEM((rows, nt), F32),
        pltpu.VMEM((B, 2*B), F32),
        pltpu.VMEM((B, 2*B), F32),
        pltpu.VMEM((2, 3*B, wide), BF),
    ]
    specs = [pl.BlockSpec(memory_space=pltpu.SMEM)] + [vmem] * (len(args) - 1)
    if first == 0:
        outs.append(real(n - last * B, n + nt - last * B))
        share = args[1].shape[1] // 2
        scratch = [pltpu.VMEM((planes * ZS, 2, share, B), F32), pltpu.VMEM((nt, n), F32)] + scratch
    else:
        specs[2] = pl.BlockSpec(memory_space=pl.ANY)
    return pl.pallas_call(
        lambda *refs: chol_kernel(first, last, n, planes, spots, *refs),
        out_shape=tuple(outs),
        in_specs=specs,
        out_specs=(vmem,) * len(outs),
        scratch_shapes=scratch,
        compiler_params=pltpu.CompilerParams(vmem_limit_bytes=32*1024*1024),
        cost_estimate=pl.CostEstimate(flops=30*n*n*n // 2, bytes_accessed=4*rows*n, transcendentals=0),
    )(*args)


def factor_kernel(info_ref, *refs):
    tiles, out_ref = refs[:-1], refs[-1]
    place, myz, myq = here(info_ref)
    row = 0
    for at in range(0, len(tiles), 2):
        rows = tiles[at].shape[0]
        out_ref[place, row:row+rows, :] = tiles[at][...]
        out_ref[1 - place, row:row+rows, :] = tiles[at+1][...]
        row += rows


DIMS = (((0,), (0,)), ((), ()))


def pivot_kernel(info_ref, piv_ref, other_ref, a_ref, *refs):
    slots, (g_ref, own_ref, done) = refs[:-3], refs[-3:]
    live, tile = other_ref.shape
    copy = pltpu.make_async_copy(piv_ref.at[0, pl.ds(0, live), :], own_ref, done)
    copy.start()
    n = a_ref.shape[1]
    place, myz, myq = here(info_ref)
    rows = lax.broadcasted_iota(jnp.int32, (live, B), 0)
    zero = jnp.zeros((live, B), BF)
    per = tile // B
    for half, ref in ((1 - place, other_ref), (place, own_ref)):
        if ref is own_ref:
            copy.wait()
        for j in range(per):
            end = info_ref[half * per + j]
            at = pl.multiple_of(half * tile + j * B, B)
            a_ref[:, pl.ds(at, B)] = jnp.where(rows < end, ref[:, j*B:(j+1)*B], zero)
    nb = n // B
    for core in range(2):
        @pl.when(place == core)
        def _():
            runs = [(j, 0, j + 1) for j in range(core, nb - 1, 2)] + [(nb - 1, 0, 2) if core == 0 else (nb - 1, 2, nb)]
            for j, low, high in runs:
                at = gram_rows(low, j, nb)[1]
                g_ref[at:at+(high-low)*B, :] = lax.dot_general(
                    a_ref[:, low*B:high*B], a_ref[:, j*B:(j+1)*B], DIMS, preferred_element_type=F32
                )
    used = nb * (nb + 1) // 4 * B
    if used < g_ref.shape[0]:
        g_ref[used:, :] = jnp.zeros((g_ref.shape[0] - used, B), F32)
    share = slots[0].shape[0] // ZS
    for q, slot in enumerate(slots):
        for z in range(ZS):
            at = pl.multiple_of((z * len(slots) + (myq ^ q)) * share, 8)
            slot[z*share:(z+1)*share, :] = g_ref[pl.ds(at, share), :]
        if q:
            slot[ZS*share:, :] = jnp.full((8, B), info_ref[info_ref.shape[0] - 4], jnp.int32).astype(F32)


def pivot_plane_kernel(info_ref, own_ref, *refs):
    got, slots = refs[:-ZS], refs[-ZS:]
    share = own_ref.shape[0] // ZS
    place, myz, myq = here(info_ref)
    parent = info_ref[info_ref.shape[0] - 4]
    theirs = [jnp.broadcast_to(ref[ZS*share:ZS*share+1, :], (share, B)) for ref in got]
    for r, slot in enumerate(slots):
        at = pl.multiple_of((myz ^ r) * share, 8)
        own = own_ref[pl.ds(at, share), :]
        parts = [ref[pl.ds(at, share), :] for ref in got]
        for p in range(NPAR):
            total = jnp.where(parent == p, own, 0.0)
            for part, their in zip(parts, theirs):
                total = total + jnp.where(their == p, part, 0.0)
            slot[p*share:(p+1)*share, :] = total


def pivot_line_kernel(info_ref, own_ref, *refs):
    got, outs = refs[:-2], refs[-2:]
    share = own_ref.shape[0] // NPAR
    place, myz, myq = here(info_ref)
    for out, p in zip(outs, (place, 1 - place)):
        at = pl.ds(pl.multiple_of(p * share, 8), share)
        total = own_ref[at, :]
        for ref in got:
            total = total + ref[at, :]
        out[...] = total


def trail_kernel(info_ref, a_ref, trail_ref, *refs):
    slots, (t_ref, own_ref, done) = refs[:-3], refs[-3:]
    live, n = a_ref.shape
    wide = trail_ref.shape[2] // ZS
    copies = [
        pltpu.make_async_copy(trail_ref.at[0, pl.ds(0, live), pl.ds(z * wide, wide)], own_ref.at[z], done.at[z]) for z in range(ZS)
    ]
    for copy in copies:
        copy.start()
    place, myz, myq = here(info_ref)
    rows = lax.broadcasted_iota(jnp.int32, (live, B), 0)
    zero = jnp.zeros((live, B), BF)
    per = trail_ref.shape[2] // B
    group = per // ZS
    width = slots[0].shape[0] // ZS
    scales = [[] for _ in slots]
    for z in range(ZS):
        copies[z].wait()
        cols = []
        for h in range(group):
            end = info_ref[n // B + place * per + z * group + h]
            cols.append(jnp.where(rows < end, own_ref[z, :, h*B:(h+1)*B], zero))
        t_ref[z % 2] = lax.dot_general(jnp.concatenate(cols, axis=1), a_ref[...], DIMS, preferred_element_type=F32)
        for q, slot in enumerate(slots):
            at = pl.multiple_of((myq ^ q) * width, width)
            part = t_ref[z % 2, pl.ds(at, width), :]
            if q:
                part, e, mant = encode(part)
                scales[q].append((e, mant))
            slot[z*width:(z+1)*width, :] = part.astype(slot.dtype)
    for q, slot in enumerate(slots):
        if q:
            spare = [jnp.full((1, n), info_ref[info_ref.shape[0] - 4], jnp.int32)]
            write_scales(slot, ZS * width, [e for e, _ in scales[q]] + [m for _, m in scales[q]] + spare)


def write_scales(slot, at, rows):
    rows = rows + [jnp.zeros_like(rows[0])] * (16 - len(rows))
    slot[at:at+16, :] = jnp.concatenate(rows, axis=0).astype(jnp.int16)


def row_of(tile, index):
    rows = lax.broadcasted_iota(jnp.int32, tile.shape, 0)
    return jnp.sum(jnp.where(rows == index, tile, 0), axis=0, keepdims=True)


def trail_plane_kernel(info_ref, own_ref, *refs):
    got, slots = refs[:-ZS], refs[-ZS:]
    width = own_ref.shape[0] // ZS
    place, myz, myq = here(info_ref)
    parent = info_ref[info_ref.shape[0] - 4]
    tiles = [ref[ZS*width:, :].astype(jnp.int32) for ref in got]
    for r, slot in enumerate(slots):
        z = myz ^ r
        at = pl.multiple_of(z * width, width)
        own = own_ref[pl.ds(at, width), :]
        parts = [ref[pl.ds(at, width), :].astype(jnp.int32).astype(F32) for ref in got]
        steps = [scale_of(row_of(tile, z), row_of(tile, ZS + z)) for tile in tiles]
        scales = []
        for p in range(NPAR):
            total = jnp.where(parent == p, own, 0.0)
            for part, step, tile in zip(parts, steps, tiles):
                total = total + part * jnp.where(tile[2*ZS:2*ZS+1, :] == p, step, 0.0)
            if r:
                total, e, mant = encode(total)
                scales.append((e, mant))
            slot[p*width:(p+1)*width, :] = total.astype(slot.dtype)
        if r:
            write_scales(slot, NPAR * width, [e for e, _ in scales] + [m for _, m in scales])


def trail_line_kernel(info_ref, own_ref, *refs):
    got, outs = refs[:-2], refs[-2:]
    width = own_ref.shape[0] // NPAR
    place, myz, myq = here(info_ref)
    tiles = [ref[NPAR*width:, :].astype(jnp.int32) for ref in got]
    for out, p in zip(outs, (place, 1 - place)):
        at = pl.ds(pl.multiple_of(p * width, width), width)
        total = own_ref[at, :]
        for ref, tile in zip(got, tiles):
            total = total + ref[at, :].astype(jnp.int32).astype(F32) * scale_of(row_of(tile, p), row_of(tile, NPAR + p))
        out[...] = total


def unpack_kernel(spots, info_ref, *refs):
    o_ref = refs[-1]
    planes = 4
    words, scales = refs[:len(spots)], refs[len(spots):2*len(spots)]
    place, myz, myq = here(info_ref)
    zs, rows, lanes = words[0].shape
    found = {(q, start + r): (at, r) for at, (q, start) in enumerate(spots) for r in range(words[at].shape[0])}
    half = lanes // 2
    lane = lax.broadcasted_iota(jnp.int32, (rows, lanes), 1)
    which = lax.broadcasted_iota(jnp.int32, (8, lanes), 0)
    blocks = pl.num_programs(0)
    odd = (myq & 1) == 1

    def values(q, r):
        at, r = found[q, r]
        steps = scale_of(*high_low(scales[at][r]))
        picked = [jnp.sum(jnp.where(which == pl.program_id(0) + h * blocks, steps, 0.0), axis=0, keepdims=True) for h in (0, 1)]
        return [v.astype(F32) * step for v, step in zip(high_low(words[at][r]), picked)]

    for q in range(0, planes, 2):
        for r in range(zs):
            at = pl.multiple_of(((myz ^ r) * planes + ((myq ^ q) & 2)) * half, lanes)
            for h, (a, b) in enumerate(zip(values(q, r), values(q + 1, r))):
                a, b = jnp.where(odd, b, a), jnp.where(odd, a, b)
                o_ref[0, 0, h, :, pl.ds(at, lanes)] = jnp.where(lane < half, a, pltpu.roll(b, half, 1))
                o_ref[1, 0, h, :, pl.ds(at, lanes)] = jnp.where(lane < half, pltpu.roll(a, half, 1), b)


def unpack(info, slots, spots, part, parts, before, wait):
    zs, rows, lanes = slots[0].shape
    rows -= 8
    wide = 4 * zs * lanes // 2
    blocks = rows // B
    args = list(slots) * 2
    specs = [pl.BlockSpec((x.shape[0], B, lanes), lambda k, info: (0, k, 0)) for x in slots]
    specs += [pl.BlockSpec((x.shape[0], 8, lanes), lambda k, info: (0, rows // 8, 0)) for x in slots]
    for extra in [before] if wait is None else [wait]:
        args.append(extra)
        specs.append(pl.BlockSpec(memory_space=pl.ANY))
    return pl.pallas_call(
        lambda *refs: unpack_kernel(spots, *refs),
        out_shape=real(NPAR, parts, 2, rows, wide),
        grid_spec=pltpu.PrefetchScalarGridSpec(
            num_scalar_prefetch=1,
            grid=(blocks,),
            in_specs=specs,
            out_specs=pl.BlockSpec((NPAR, 1, 2, B, wide), lambda k, info: (0, part, 0, k, 0)),
        ),
        input_output_aliases={} if before is None else {len(args): 0},
        compiler_params=pltpu.CompilerParams(vmem_limit_bytes=32*1024*1024),
        cost_estimate=pl.CostEstimate(flops=0, bytes_accessed=20*rows*wide, transcendentals=0),
    )(info, *args)


def unpack_plain(q):
    chips, rows, lanes = q.shape
    rows -= 8
    blocks = rows // B
    step = scale_of(*high_low(q[:, rows:rows+2*blocks])).reshape(chips, 2, blocks, 1, lanes)
    z = jnp.stack(high_low(q[:, :rows]), axis=1).astype(F32).reshape(chips, 2, blocks, B, lanes) * step
    z = z.reshape(chips, 2 * rows, NPAR, lanes // NPAR)
    return jnp.transpose(z, (2, 1, 0, 3)).reshape(NPAR, 2 * rows, chips * lanes // NPAR)


def shards(count, piv_cols, trail_cols, row_end, parent_of):
    place = lax.axis_index("front")
    me = lax.axis_index("sub")
    planes = count // ZS
    myz, myq = me // planes, me % planes
    tile_pivot, tile_trail = piv_cols.shape[2], trail_cols.shape[2]
    n = NPAR * tile_pivot
    width = tile_trail // count
    nb = n // B
    share = -(-(nb * (nb + 1) // 4 * B) // (8 * count)) * 8

    def flip(x, mask):
        return lax.ppermute(x, "sub", [(i, i ^ mask) for i in range(count)])

    def over_plane(slots):
        return [flip(x, q) for q, x in enumerate(slots) if q]

    def over_line(slots):
        return [flip(x, r * planes) for r, x in enumerate(slots) if r]

    def everywhere(x):
        line = jnp.stack([x] + over_line([x] * ZS))
        if planes != 4:
            return [line] + over_plane([line] * planes)
        one, two = flip(line, 1), flip(line, 2)
        return [line, one, two, flip(one[:ZS//2], 2), flip(two[ZS//2:], 1)]

    spots = [(q, 0) for q in range(planes)]
    if planes == 4:
        spots = spots + [(3, ZS // 2)]

    other_piv = lax.ppermute(piv_cols[0, :LIVE], "front", SWAP)
    info = jnp.concatenate([row_end[0], parent_of, jnp.stack([place, myz, myq]).astype(jnp.int32)])

    outs = [jax.ShapeDtypeStruct((LIVE, n), BF), real(ZS * share, B)] + [real(ZS * share + 8, B)] * (planes - 1)
    masked, *slots = call(
        pivot_kernel, info, (piv_cols, other_piv), outs,
        [pltpu.VMEM((count * share, B), F32), pltpu.VMEM((LIVE, tile_pivot), BF), pltpu.SemaphoreType.DMA],
        far=(0,), cost=LIVE*n*n,
    )
    got = over_plane(slots)
    outs = [real(ZS * width, n)] + [short(ZS * width + 16, n)] * (planes - 1)
    trails = call(
        trail_kernel, info, (masked, trail_cols), outs,
        [pltpu.VMEM((2, planes * width, n), F32), pltpu.VMEM((ZS, LIVE, tile_trail // ZS), BF), pltpu.SemaphoreType.DMA((ZS,))],
        far=(1,), cost=2*LIVE*n*tile_trail, limit=32,
    )
    got_trails = over_plane(trails)

    slots = call(pivot_plane_kernel, info, (slots[0], *got), [real(NPAR * share, B)] * ZS)
    keep, give = call(pivot_line_kernel, info, (slots[0], *over_line(slots)), [real(share, B)] * 2)
    grams = everywhere(jnp.concatenate([keep, lax.ppermute(give, "front", SWAP)], axis=0))

    outs = [real(NPAR * width, n)] + [short(NPAR * width + 16, n)] * (ZS - 1)
    trails = call(trail_plane_kernel, info, (trails[0], *got_trails), outs)
    keep, give = call(trail_line_kernel, info, (trails[0], *over_line(trails)), [real(width, n)] * 2)
    got = lax.ppermute(give, "front", SWAP)

    def gather(codes):
        theirs = lax.ppermute(codes, "front", SWAP)
        return jnp.where(
            place == 0,
            jnp.concatenate([codes[:, :width], theirs[:, :width]], axis=1),
            jnp.concatenate([theirs[:, width:], codes[:, width:]], axis=1),
        )

    def in_order(slots):
        every = jnp.stack(slots)
        every = jnp.take(jnp.take(every, jnp.arange(planes) ^ myq, axis=0), jnp.arange(ZS) ^ myz, axis=1)
        return jnp.swapaxes(every, 0, 1).reshape((count,) + every.shape[2:])

    r_keep, give, codes, rest = chol_rows(0, nb // 2, n, NPAR * width, planes, spots, info, *grams, keep, got)
    tiles = [r_keep, lax.ppermute(give, "front", SWAP)]
    words = gather(codes)
    first = everywhere(words)
    r_keep, give, codes = chol_rows(nb // 2, nb, n, NPAR * width, planes, spots, info, rest, words)
    tiles += [r_keep, lax.ppermute(give, "front", SWAP)]
    second = everywhere(gather(codes))
    (r_pivot,) = call(factor_kernel, info, tiles, [real(NPAR, n, tile_pivot)], limit=32)
    if 2 * width == B and planes == 4:
        r_trail = unpack(info, first, spots, 0, 2, None, r_pivot)
        r_trail = unpack(info, second, spots, 1, 2, r_trail, None).reshape(NPAR, n, -1)
    else:
        r_trail = jnp.concatenate([unpack_plain(in_order(first)), unpack_plain(in_order(second))], axis=1)
    return (r_pivot, r_trail)


def solution(mesh):
    count = mesh.shape["sub"]
    return jax.shard_map(
        lambda *args: shards(count, *args),
        mesh=mesh,
        in_specs=(P("sub", None, "front"), P("sub", None, "front"), P("sub", None), P("sub")),
        out_specs=(P(None, None, "front"), P(None, None, "front")),
        check_vma=False,
    )
```

```python
import jax, jax.numpy as jnp
from jax import lax
from jax.experimental import pallas as pl
from jax.experimental.pallas import tpu as pltpu
from jax.sharding import PartitionSpec as P
B=128
F32=jnp.float32
BF=jnp.bfloat16
LIVE = 1280
NPAR = 2
ZS = 4
LEVELS = 32766.0
SWAP = [(0, 1), (1, 0)]

def split(x):
    hi = x.astype(BF)
    return hi, (x - hi.astype(F32)).astype(BF)

def factor_block(d_ref, w_ref, fillers):
    rows8 = (8, B)
    for g in range(B // 8):
        xs, xi = [], []
        for i in range(8):
            row = d_ref[8*g+i:8*g+i+1, :]
            xs.append(jnp.broadcast_to(row[:, :B], rows8))
            xi.append(jnp.broadcast_to(row[:, B:], rows8))
        s = {}
        for i in range(8):
            for j in range(i, 8):
                s[i, j] = jnp.broadcast_to(xs[i][:, 8*g+j:8*g+j+1], rows8)
        after = 8 * (g + 1)
        if after < B:
            blk = d_ref[after:after+8, :B]
            bi = d_ref[after:after+8, B:]
            cols = [jnp.broadcast_to(blk[:, 8*g+i:8*g+i+1], rows8) for i in range(8)]
        for i in range(8):
            rs = lax.rsqrt(s[i, i])
            inv = rs * rs
            w_ref[8*g+i:8*g+i+1, :B] = (xs[i] * rs)[:1]
            w_ref[8*g+i:8*g+i+1, B:] = (xi[i] * rs)[:1]
            for r in range(8):
                if r == i: continue
                m = (s[r, i] if r < i else s[i, r]) * inv
                for j in range(max(r, i+1), 8):
                    s[r, j] = s[r, j] - m * s[i, j]
                xs[r] = xs[r] - m * xs[i]
                xi[r] = xi[r] - m * xi[i]
            s[i, i] = inv
            if after < B:
                m = cols[i] * inv
                blk = blk - m * xs[i]
                bi = bi - m * xi[i]
                for j in range(i+1, 8):
                    cols[j] = cols[j] - m * s[i, j]
        if after < B:
            d_ref[after:after+8, :B] = blk
            d_ref[after:after+8, B:] = bi
        ys = [xs[i] * s[i, i] for i in range(8)]
        yi = [xi[i] * s[i, i] for i in range(8)]
        for r in range(g+2, B // 8):
            blk = d_ref[8*r:8*r+8, :B]
            bi = d_ref[8*r:8*r+8, B:]
            cols = [jnp.broadcast_to(blk[:, 8*g+i:8*g+i+1], rows8) for i in range(8)]
            for i in range(8):
                blk = blk - cols[i] * ys[i]
                bi = bi - cols[i] * yi[i]
            d_ref[8*r:8*r+8, :B] = blk
            d_ref[8*r:8*r+8, B:] = bi
        if fillers:
            fillers.pop(0)()
    while fillers:
        fillers.pop(0)()


def gram_rows(i, j, nb):
    t = j // 2
    if j == nb - 1:
        return (0, (t * t + 2 * t + 1 + i) * B) if i < 2 else (1, (t * t + t + i - 2) * B)
    return j % 2, (t * t + (j % 2) * t + i) * B


def chol_kernel(first, last, n, planes, spots, *refs):
    begin = first == 0
    info_ref, *refs = refs
    place, myz, myq = here(info_ref)
    if begin:
        slots, (keep_ref, got_ref), refs = refs[:len(spots)], refs[len(spots):len(spots)+2], refs[len(spots)+2:]
    else:
        in_ref, _, _, *refs = refs
    r_keep_ref, r_give_ref, q_ref, *refs = refs
    if begin:
        out_ref, g_ref, t_ref, *refs = refs
        share = g_ref.shape[2]
        for slot, (q, start) in zip(slots, spots):
            for r in range(slot.shape[0]):
                chip = (myz ^ (start + r)) * planes + (myq ^ q)
                for c in range(2):
                    g_ref[chip, place ^ c] = slot[r, c*share:(c+1)*share, :]
        wide = keep_ref.shape[0]
        t_ref[pl.ds(pl.multiple_of(place * wide, wide), wide), :] = keep_ref[...]
        t_ref[pl.ds(pl.multiple_of((1 - place) * wide, wide), wide), :] = got_ref[...]
    r_ref, s_ref, z_ref, d_ref, w_ref, rhs_ref = refs
    nt = z_ref.shape[1]
    nb = n // B
    base = first * B
    ri = lax.broadcasted_iota(jnp.int32, (B, B), 0)
    ci = lax.broadcasted_iota(jnp.int32, (B, B), 1)

    def gram_parts(i, j):
        core, at = gram_rows(i, j, nb)
        share = g_ref.shape[2]
        end, row = at + B, 0
        while at < end:
            chip, off = at // share, at % share
            size = min(share - off, end - at)
            yield row, g_ref[chip, core, off:off+size, :]
            at, row = at + size, row + size

    def load(k, lo, hi):
        if not begin:
            return in_ref[(k-first)*B:(k-first+1)*B, lo-base:hi-base]
        for j in range(lo // B, min(hi, n) // B):
            for row, part in gram_parts(k, j):
                s_ref[k*B+row:k*B+row+part.shape[0], j*B:(j+1)*B] = part
        if hi > n:
            s_ref[k*B:(k+1)*B, n:] = jnp.transpose(t_ref[:, k*B:(k+1)*B])
        return s_ref[k*B:(k+1)*B, lo:hi]

    def current(k, lo, hi):
        return load(k, lo, hi) if k == first else s_ref[k*B-base:(k+1)*B-base, lo-base:hi-base]

    def update(k, i):
        def run():
            lo = i * B
            lhs = split(jnp.transpose(r_ref[k*B-base:(k+1)*B-base, lo:lo+B]))
            lhs = jnp.concatenate([lhs[0], lhs[0], lhs[1]], axis=1)
            upd = jnp.dot(lhs, rhs_ref[k % 2, :, lo-base:], preferred_element_type=F32)
            if i >= last and k == last - 1:
                out_ref[(i-last)*B:(i-last+1)*B, lo-last*B:] = s_ref[lo-base:lo-base+B, lo-base:] - upd
            elif k > first:
                s_ref[lo-base:lo-base+B, lo-base:] = s_ref[lo-base:lo-base+B, lo-base:] - upd
            elif begin:
                for j in range(i, nb):
                    for row, part in gram_parts(i, j):
                        size = part.shape[0]
                        s_ref[lo+row:lo+row+size, j*B:(j+1)*B] = part - upd[row:row+size, (j-i)*B:(j-i+1)*B]
                s_ref[lo:lo+B, n:] = jnp.transpose(t_ref[:, lo:lo+B]) - upd[:, n-lo:]
            else:
                s_ref[lo-base:lo-base+B, lo-base:] = in_ref[lo-base:lo-base+B, lo-base:] - upd
        return run

    fillers = []
    for k in range(first, last):
        lo = k * B
        at = lo - base
        d_ref[:, :B] = current(k, lo, lo + B)
        d_ref[:, B:] = jnp.where(ri == ci, 1.0, 0.0).astype(F32)
        factor_block(d_ref, w_ref, fillers)
        fillers = []
        if k:
            r_ref[at:at+B, :lo] = jnp.zeros((B, lo), F32)
        r_ref[at:at+B, lo:lo+B] = jnp.where(ci >= ri, w_ref[:, :B], 0.0)
        wh, wl = split(w_ref[:, B:])
        w3 = jnp.concatenate([wh, wh, wl], axis=1)
        rh, rl = split(current(k, lo + B, n + nt))
        p = jnp.dot(w3, jnp.concatenate([rh, rl, rh], axis=0), preferred_element_type=F32)
        if k < nb - 1:
            r_ref[at:at+B, lo+B:] = p[:, :n-lo-B]
        z_ref[at:at+B, :] = p[:, n-lo-B:]
        ph, pll = split(p)
        rhs_ref[k % 2, 0:B, lo+B-base:] = ph
        rhs_ref[k % 2, B:2*B, lo+B-base:] = pll
        rhs_ref[k % 2, 2*B:, lo+B-base:] = ph
        if k < nb - 1:
            update(k, k+1)()
            fillers = [update(k, i) for i in range(k+2, nb)]
    for fill in fillers:
        fill()
    tile = r_keep_ref.shape[1]
    r_keep_ref[...] = r_ref[:, pl.ds(pl.multiple_of(place * tile, B), tile)]
    r_give_ref[...] = r_ref[:, pl.ds(pl.multiple_of((1 - place) * tile, B), tile)]
    count = last - first
    coded = [encode(z_ref[k*B:(k+1)*B, :]) for k in range(count)]
    for k in range(count // 2):
        q_ref[k*B:(k+1)*B, :] = join(coded[k][0], coded[k + count // 2][0])
    scales = [join(e, mant) for _, e, mant in coded]
    scales += [jnp.zeros_like(scales[0])] * (8 - count)
    q_ref[count//2*B:, :] = jnp.concatenate(scales, axis=0)


def here(info_ref):
    end = info_ref.shape[0]
    return info_ref[end - 3], info_ref[end - 2], info_ref[end - 1]


def scale_of(e, mant):
    return mant.astype(F32) * jnp.exp2(e.astype(F32)) * (1.0 / (16384.0 * LEVELS))


def encode(x):
    top = jnp.maximum(jnp.max(jnp.abs(x), axis=0, keepdims=True), 1e-30)
    e = jnp.ceil(jnp.log2(top)).astype(jnp.int32)
    mant = jnp.minimum(jnp.ceil(top * jnp.exp2(-e.astype(F32)) * 16384.0) + 1.0, 32767.0).astype(jnp.int32)
    codes = jnp.clip(jnp.round(x * (1.0 / scale_of(e, mant))), -LEVELS, LEVELS)
    return codes.astype(jnp.int32), e, mant


def join(high, low):
    return jnp.bitwise_or(jnp.left_shift(high, 16), jnp.bitwise_and(low, 65535))


def high_low(word):
    return jnp.right_shift(word, 16), jnp.right_shift(jnp.left_shift(word, 16), 16)


def call(kernel, info, args, outs, scratch=(), far=(), cost=0, limit=24, through=0):
    still = pl.BlockSpec(memory_space=pl.ANY)
    kept, made = len(args) - through, len(outs)
    far = tuple(far) + tuple(range(kept, len(args)))
    passed = [jax.ShapeDtypeStruct(arg.shape, arg.dtype) for arg in args[kept:]]
    return pl.pallas_call(
        kernel,
        out_shape=tuple(outs) + tuple(passed),
        grid_spec=pltpu.PrefetchScalarGridSpec(
            num_scalar_prefetch=1,
            grid=(1,),
            in_specs=[
                still if at in far else pl.BlockSpec(arg.shape, lambda i, info, zeros=(0,) * len(arg.shape): zeros)
                for at, arg in enumerate(args)
            ],
            out_specs=tuple(pl.BlockSpec(out.shape, lambda i, info, zeros=(0,) * len(out.shape): zeros) for out in outs) + (still,) * through,
            scratch_shapes=list(scratch),
        ),
        input_output_aliases={1 + kept + i: made + i for i in range(through)},
        compiler_params=pltpu.CompilerParams(vmem_limit_bytes=limit*1024*1024),
        cost_estimate=pl.CostEstimate(flops=cost, bytes_accessed=4*1024*1024, transcendentals=0),
    )(info, *args)


def real(*shape):
    return jax.ShapeDtypeStruct(shape, F32)


def short(*shape):
    return jax.ShapeDtypeStruct(shape, jnp.int16)


def chol_rows(first, last, n, nt, planes, spots, *args):
    vmem = pl.BlockSpec(memory_space=pltpu.VMEM)
    rows = (last - first) * B
    wide = n + nt - first * B
    outs = [real(rows, n // 2), real(rows, n // 2), jax.ShapeDtypeStruct((rows // 2 + 8, nt), jnp.int32)]
    scratch = [
        pltpu.VMEM((rows, n), F32),
        pltpu.VMEM((n - first * B, wide), F32),
        pltpu.VMEM((rows, nt), F32),
        pltpu.VMEM((B, 2*B), F32),
        pltpu.VMEM((B, 2*B), F32),
        pltpu.VMEM((2, 3*B, wide), BF),
    ]
    specs = [pl.BlockSpec(memory_space=pltpu.SMEM)] + [vmem] * (len(args) - 1)
    if first == 0:
        outs.append(real(n - last * B, n + nt - last * B))
        share = args[1].shape[1] // 2
        scratch = [pltpu.VMEM((planes * ZS, 2, share, B), F32), pltpu.VMEM((nt, n), F32)] + scratch
    else:
        specs[2:] = [pl.BlockSpec(memory_space=pl.ANY)] * 2
    return pl.pallas_call(
        lambda *refs: chol_kernel(first, last, n, planes, spots, *refs),
        out_shape=tuple(outs),
        in_specs=specs,
        out_specs=(vmem,) * len(outs),
        scratch_shapes=scratch,
        compiler_params=pltpu.CompilerParams(vmem_limit_bytes=32*1024*1024),
        cost_estimate=pl.CostEstimate(flops=30*n*n*n // 2, bytes_accessed=4*rows*n, transcendentals=0),
    )(*args)


def factor_kernel(info_ref, *refs):
    tiles, out_ref = refs[:-1], refs[-1]
    place, myz, myq = here(info_ref)
    row = 0
    for at in range(0, len(tiles), 2):
        rows = tiles[at].shape[0]
        out_ref[place, row:row+rows, :] = tiles[at][...]
        out_ref[1 - place, row:row+rows, :] = tiles[at+1][...]
        row += rows


DIMS = (((0,), (0,)), ((), ()))


def pivot_kernel(info_ref, own_ref, other_ref, a_ref, *refs):
    slots, g_ref = refs[:-1], refs[-1]
    live, tile = other_ref.shape
    n = a_ref.shape[1]
    place, myz, myq = here(info_ref)
    rows = lax.broadcasted_iota(jnp.int32, (live, B), 0)
    zero = jnp.zeros((live, B), BF)
    per = tile // B
    for half, ref in ((place, own_ref), (1 - place, other_ref)):
        for j in range(per):
            end = info_ref[half * per + j]
            at = pl.multiple_of(half * tile + j * B, B)
            a_ref[:, pl.ds(at, B)] = jnp.where(rows < end, ref[:, j*B:(j+1)*B], zero)
    nb = n // B
    for core in range(2):
        @pl.when(place == core)
        def _():
            runs = [(j, 0, j + 1) for j in range(core, nb - 1, 2)] + [(nb - 1, 0, 2) if core == 0 else (nb - 1, 2, nb)]
            for j, low, high in runs:
                at = gram_rows(low, j, nb)[1]
                g_ref[at:at+(high-low)*B, :] = lax.dot_general(
                    a_ref[:, low*B:high*B], a_ref[:, j*B:(j+1)*B], DIMS, preferred_element_type=F32
                )
    used = nb * (nb + 1) // 4 * B
    if used < g_ref.shape[0]:
        g_ref[used:, :] = jnp.zeros((g_ref.shape[0] - used, B), F32)
    share = slots[0].shape[0] // ZS
    for q, slot in enumerate(slots):
        for z in range(ZS):
            at = pl.multiple_of((z * len(slots) + (myq ^ q)) * share, 8)
            slot[z*share:(z+1)*share, :] = g_ref[pl.ds(at, share), :]
        if q:
            slot[ZS*share:, :] = jnp.full((8, B), info_ref[info_ref.shape[0] - 4], jnp.int32).astype(F32)


def pivot_plane_kernel(planes, info_ref, own_ref, *refs):
    got, slots = refs[:planes-1], refs[2*(planes-1):2*(planes-1)+ZS]
    share = own_ref.shape[0] // ZS
    place, myz, myq = here(info_ref)
    parent = info_ref[info_ref.shape[0] - 4]
    theirs = [jnp.broadcast_to(ref[ZS*share:ZS*share+1, :], (share, B)) for ref in got]
    for r, slot in enumerate(slots):
        at = pl.multiple_of((myz ^ r) * share, 8)
        own = own_ref[pl.ds(at, share), :]
        parts = [ref[pl.ds(at, share), :] for ref in got]
        for p in range(NPAR):
            total = jnp.where(parent == p, own, 0.0)
            for part, their in zip(parts, theirs):
                total = total + jnp.where(their == p, part, 0.0)
            slot[p*share:(p+1)*share, :] = total


def pivot_line_kernel(info_ref, own_ref, *refs):
    got, outs = refs[:ZS-1], refs[-2:]
    share = own_ref.shape[0] // NPAR
    place, myz, myq = here(info_ref)
    for out, p in zip(outs, (place, 1 - place)):
        at = pl.ds(pl.multiple_of(p * share, 8), share)
        total = own_ref[at, :]
        for ref in got:
            total = total + ref[at, :]
        out[...] = total


def trail_kernel(info_ref, a_ref, trail_ref, *refs):
    slots, (t_ref, own_ref, done) = refs[:-3], refs[-3:]
    live, n = a_ref.shape
    wide = trail_ref.shape[2] // ZS
    copies = [
        pltpu.make_async_copy(trail_ref.at[0, pl.ds(0, live), pl.ds(z * wide, wide)], own_ref.at[z], done.at[z]) for z in range(ZS)
    ]
    for copy in copies:
        copy.start()
    place, myz, myq = here(info_ref)
    rows = lax.broadcasted_iota(jnp.int32, (live, B), 0)
    zero = jnp.zeros((live, B), BF)
    per = trail_ref.shape[2] // B
    group = per // ZS
    width = slots[0].shape[0] // ZS
    scales = [[] for _ in slots]
    for z in range(ZS):
        copies[z].wait()
        cols = []
        for h in range(group):
            end = info_ref[n // B + place * per + z * group + h]
            cols.append(jnp.where(rows < end, own_ref[z, :, h*B:(h+1)*B], zero))
        t_ref[z % 2] = lax.dot_general(jnp.concatenate(cols, axis=1), a_ref[...], DIMS, preferred_element_type=F32)
        for q, slot in enumerate(slots):
            at = pl.multiple_of((myq ^ q) * width, width)
            part = t_ref[z % 2, pl.ds(at, width), :]
            if q:
                part, e, mant = encode(part)
                scales[q].append((e, mant))
            slot[z*width:(z+1)*width, :] = part.astype(slot.dtype)
    for q, slot in enumerate(slots):
        if q:
            spare = [jnp.full((1, n), info_ref[info_ref.shape[0] - 4], jnp.int32)]
            write_scales(slot, ZS * width, [e for e, _ in scales[q]] + [m for _, m in scales[q]] + spare)


def write_scales(slot, at, rows):
    rows = rows + [jnp.zeros_like(rows[0])] * (16 - len(rows))
    slot[at:at+16, :] = jnp.concatenate(rows, axis=0).astype(jnp.int16)


def row_of(tile, index):
    rows = lax.broadcasted_iota(jnp.int32, tile.shape, 0)
    return jnp.sum(jnp.where(rows == index, tile, 0), axis=0, keepdims=True)


def trail_plane_kernel(info_ref, own_ref, *refs):
    got, slots = refs[:-ZS], refs[-ZS:]
    width = own_ref.shape[0] // ZS
    place, myz, myq = here(info_ref)
    parent = info_ref[info_ref.shape[0] - 4]
    tiles = [ref[ZS*width:, :].astype(jnp.int32) for ref in got]
    for r, slot in enumerate(slots):
        z = myz ^ r
        at = pl.multiple_of(z * width, width)
        own = own_ref[pl.ds(at, width), :]
        parts = [ref[pl.ds(at, width), :].astype(jnp.int32).astype(F32) for ref in got]
        steps = [scale_of(row_of(tile, z), row_of(tile, ZS + z)) for tile in tiles]
        scales = []
        for p in range(NPAR):
            total = jnp.where(parent == p, own, 0.0)
            for part, step, tile in zip(parts, steps, tiles):
                total = total + part * jnp.where(tile[2*ZS:2*ZS+1, :] == p, step, 0.0)
            if r:
                total, e, mant = encode(total)
                scales.append((e, mant))
            slot[p*width:(p+1)*width, :] = total.astype(slot.dtype)
        if r:
            write_scales(slot, NPAR * width, [e for e, _ in scales] + [m for _, m in scales])


def trail_line_kernel(info_ref, own_ref, *refs):
    got, outs = refs[:-2], refs[-2:]
    width = own_ref.shape[0] // NPAR
    place, myz, myq = here(info_ref)
    tiles = [ref[NPAR*width:, :].astype(jnp.int32) for ref in got]
    for out, p in zip(outs, (place, 1 - place)):
        at = pl.ds(pl.multiple_of(p * width, width), width)
        total = own_ref[at, :]
        for ref, tile in zip(got, tiles):
            total = total + ref[at, :].astype(jnp.int32).astype(F32) * scale_of(row_of(tile, p), row_of(tile, NPAR + p))
        out[...] = total


def unpack_kernel(spots, info_ref, *refs):
    o_ref = refs[-1]
    planes = 4
    words, scales = refs[:len(spots)], refs[len(spots):2*len(spots)]
    place, myz, myq = here(info_ref)
    zs, rows, lanes = words[0].shape
    found = {(q, start + r): (at, r) for at, (q, start) in enumerate(spots) for r in range(words[at].shape[0])}
    half = lanes // 2
    lane = lax.broadcasted_iota(jnp.int32, (rows, lanes), 1)
    which = lax.broadcasted_iota(jnp.int32, (8, lanes), 0)
    blocks = pl.num_programs(0)
    odd = (myq & 1) == 1

    def values(q, r):
        at, r = found[q, r]
        steps = scale_of(*high_low(scales[at][r]))
        picked = [jnp.sum(jnp.where(which == pl.program_id(0) + h * blocks, steps, 0.0), axis=0, keepdims=True) for h in (0, 1)]
        return [v.astype(F32) * step for v, step in zip(high_low(words[at][r]), picked)]

    for q in range(0, planes, 2):
        for r in range(zs):
            at = pl.multiple_of(((myz ^ r) * planes + ((myq ^ q) & 2)) * half, lanes)
            for h, (a, b) in enumerate(zip(values(q, r), values(q + 1, r))):
                a, b = jnp.where(odd, b, a), jnp.where(odd, a, b)
                o_ref[0, 0, h, :, pl.ds(at, lanes)] = jnp.where(lane < half, a, pltpu.roll(b, half, 1))
                o_ref[1, 0, h, :, pl.ds(at, lanes)] = jnp.where(lane < half, pltpu.roll(a, half, 1), b)


def unpack(info, slots, spots, part, parts, *behind):
    zs, rows, lanes = slots[0].shape
    rows -= 8
    wide = 4 * zs * lanes // 2
    blocks = rows // B
    args = list(slots) * 2
    specs = [pl.BlockSpec((x.shape[0], B, lanes), lambda k, info: (0, k, 0)) for x in slots]
    specs += [pl.BlockSpec((x.shape[0], 8, lanes), lambda k, info: (0, rows // 8, 0)) for x in slots]
    for extra in behind:
        args.append(extra)
        specs.append(pl.BlockSpec(memory_space=pl.ANY))
    return pl.pallas_call(
        lambda *refs: unpack_kernel(spots, *refs),
        out_shape=real(NPAR, parts, 2, rows, wide),
        grid_spec=pltpu.PrefetchScalarGridSpec(
            num_scalar_prefetch=1,
            grid=(blocks,),
            in_specs=specs,
            out_specs=pl.BlockSpec((NPAR, 1, 2, B, wide), lambda k, info: (0, part, 0, k, 0)),
        ),
        input_output_aliases={2 * len(slots) + 1: 0} if part else {},
        compiler_params=pltpu.CompilerParams(vmem_limit_bytes=32*1024*1024),
        cost_estimate=pl.CostEstimate(flops=0, bytes_accessed=20*rows*wide, transcendentals=0),
    )(info, *args)


def unpack_plain(q):
    chips, rows, lanes = q.shape
    rows -= 8
    blocks = rows // B
    step = scale_of(*high_low(q[:, rows:rows+2*blocks])).reshape(chips, 2, blocks, 1, lanes)
    z = jnp.stack(high_low(q[:, :rows]), axis=1).astype(F32).reshape(chips, 2, blocks, B, lanes) * step
    z = z.reshape(chips, 2 * rows, NPAR, lanes // NPAR)
    return jnp.transpose(z, (2, 1, 0, 3)).reshape(NPAR, 2 * rows, chips * lanes // NPAR)


def shards(count, piv_cols, trail_cols, row_end, parent_of):
    place = lax.axis_index("front")
    me = lax.axis_index("sub")
    planes = count // ZS
    myz, myq = me // planes, me % planes
    tile_pivot, tile_trail = piv_cols.shape[2], trail_cols.shape[2]
    n = NPAR * tile_pivot
    width = tile_trail // count
    nb = n // B
    share = -(-(nb * (nb + 1) // 4 * B) // (8 * count)) * 8

    def flip(x, mask):
        return lax.ppermute(x, "sub", [(i, i ^ mask) for i in range(count)])

    def over_plane(slots):
        return [flip(x, q) for q, x in enumerate(slots) if q]

    def over_line(slots):
        return [flip(x, r * planes) for r, x in enumerate(slots) if r]

    def everywhere(x):
        line = jnp.stack([x] + over_line([x] * ZS))
        if planes != 4:
            return [line] + over_plane([line] * planes)
        one, two = flip(line, 1), flip(line, 2)
        return [line, one, two, flip(one[:ZS//2], 2), flip(two[ZS//2:], 1)]

    spots = [(q, 0) for q in range(planes)]
    if planes == 4:
        spots = spots + [(3, ZS // 2)]

    own_piv = piv_cols[0, :LIVE]
    other_piv = lax.ppermute(own_piv, "front", SWAP)
    info = jnp.concatenate([row_end[0], parent_of, jnp.stack([place, myz, myq]).astype(jnp.int32)])

    outs = [jax.ShapeDtypeStruct((LIVE, n), BF), real(ZS * share, B)] + [real(ZS * share + 8, B)] * (planes - 1)
    masked, *slots = call(
        pivot_kernel, info, (own_piv, other_piv), outs,
        [pltpu.VMEM((count * share, B), F32)], cost=LIVE*n*n,
    )
    got = over_plane(slots)
    outs = [real(ZS * width, n)] + [short(ZS * width + 16, n)] * (planes - 1)
    trails = call(
        trail_kernel, info, (masked, trail_cols), outs,
        [pltpu.VMEM((2, planes * width, n), F32), pltpu.VMEM((ZS, LIVE, tile_trail // ZS), BF), pltpu.SemaphoreType.DMA((ZS,))],
        far=(1,), cost=2*LIVE*n*tile_trail, limit=32,
    )
    out = call(
        lambda *refs: pivot_plane_kernel(planes, *refs), info, (slots[0], *got, *trails[1:]), [real(NPAR * share, B)] * ZS,
        through=planes-1,
    )
    slots, trails = out[:ZS], [trails[0], *out[ZS:]]
    got_trails = over_plane(trails)
    ahead = got_trails[:2]
    keep, give = call(
        pivot_line_kernel, info, (slots[0], *over_line(slots), *ahead), [real(share, B)] * 2, far=range(ZS, ZS + len(ahead))
    )
    grams = everywhere(jnp.concatenate([keep, lax.ppermute(give, "front", SWAP)], axis=0))

    outs = [real(NPAR * width, n)] + [short(NPAR * width + 16, n)] * (ZS - 1)
    trails = call(trail_plane_kernel, info, (trails[0], *got_trails), outs)
    keep, give = call(trail_line_kernel, info, (trails[0], *over_line(trails)), [real(width, n)] * 2)
    got = lax.ppermute(give, "front", SWAP)

    def gather(codes):
        theirs = lax.ppermute(codes, "front", SWAP)
        return jnp.where(
            place == 0,
            jnp.concatenate([codes[:, :width], theirs[:, :width]], axis=1),
            jnp.concatenate([theirs[:, width:], codes[:, width:]], axis=1),
        )

    def in_order(slots):
        every = jnp.stack(slots)
        every = jnp.take(jnp.take(every, jnp.arange(planes) ^ myq, axis=0), jnp.arange(ZS) ^ myz, axis=1)
        return jnp.swapaxes(every, 0, 1).reshape((count,) + every.shape[2:])

    r_keep, give, codes, rest = chol_rows(0, nb // 2, n, NPAR * width, planes, spots, info, *grams, keep, got)
    tiles = [r_keep, lax.ppermute(give, "front", SWAP)]
    words = gather(codes)
    first = everywhere(words)
    r_keep, give, codes = chol_rows(nb // 2, nb, n, NPAR * width, planes, spots, info, rest, words, tiles[1])
    tiles += [r_keep, lax.ppermute(give, "front", SWAP)]
    second = everywhere(gather(codes))
    (r_pivot,) = call(factor_kernel, info, tiles, [real(NPAR, n, tile_pivot)], limit=32)
    if 2 * width == B and planes == 4:
        r_trail = unpack(info, first, spots, 0, 2)
        r_trail = unpack(info, second, spots, 1, 2, r_trail, r_pivot).reshape(NPAR, n, -1)
    else:
        r_trail = jnp.concatenate([unpack_plain(in_order(first)), unpack_plain(in_order(second))], axis=1)
    return (r_pivot, r_trail)


def solution(mesh):
    count = mesh.shape["sub"]
    return jax.shard_map(
        lambda *args: shards(count, *args),
        mesh=mesh,
        in_specs=(P("sub", None, "front"), P("sub", None, "front"), P("sub", None), P("sub")),
        out_specs=(P(None, None, "front"), P(None, None, "front")),
        check_vma=False,
    )
```

```python
import jax, jax.numpy as jnp
from jax import lax
from jax.experimental import pallas as pl
from jax.experimental.pallas import tpu as pltpu
from jax.sharding import PartitionSpec as P
B=128
F32=jnp.float32
BF=jnp.bfloat16
LIVE = 1280
NPAR = 2
ZS = 4
LEVELS = 32766.0
SWAP = [(0, 1), (1, 0)]

def split(x):
    hi = x.astype(BF)
    return hi, (x - hi.astype(F32)).astype(BF)

def factor_block(d_ref, w_ref, fillers):
    rows8 = (8, B)
    for g in range(B // 8):
        xs, xi = [], []
        for i in range(8):
            row = d_ref[8*g+i:8*g+i+1, :]
            xs.append(jnp.broadcast_to(row[:, :B], rows8))
            xi.append(jnp.broadcast_to(row[:, B:], rows8))
        s = {}
        for i in range(8):
            for j in range(i, 8):
                s[i, j] = jnp.broadcast_to(xs[i][:, 8*g+j:8*g+j+1], rows8)
        after = 8 * (g + 1)
        if after < B:
            blk = d_ref[after:after+8, :B]
            bi = d_ref[after:after+8, B:]
            cols = [jnp.broadcast_to(blk[:, 8*g+i:8*g+i+1], rows8) for i in range(8)]
        for i in range(8):
            rs = lax.rsqrt(s[i, i])
            inv = rs * rs
            w_ref[8*g+i:8*g+i+1, :B] = (xs[i] * rs)[:1]
            w_ref[8*g+i:8*g+i+1, B:] = (xi[i] * rs)[:1]
            for r in range(8):
                if r == i: continue
                m = (s[r, i] if r < i else s[i, r]) * inv
                for j in range(max(r, i+1), 8):
                    s[r, j] = s[r, j] - m * s[i, j]
                xs[r] = xs[r] - m * xs[i]
                xi[r] = xi[r] - m * xi[i]
            s[i, i] = inv
            if after < B:
                m = cols[i] * inv
                blk = blk - m * xs[i]
                bi = bi - m * xi[i]
                for j in range(i+1, 8):
                    cols[j] = cols[j] - m * s[i, j]
        if after < B:
            d_ref[after:after+8, :B] = blk
            d_ref[after:after+8, B:] = bi
        ys = [xs[i] * s[i, i] for i in range(8)]
        yi = [xi[i] * s[i, i] for i in range(8)]
        for r in range(g+2, B // 8):
            blk = d_ref[8*r:8*r+8, :B]
            bi = d_ref[8*r:8*r+8, B:]
            cols = [jnp.broadcast_to(blk[:, 8*g+i:8*g+i+1], rows8) for i in range(8)]
            for i in range(8):
                blk = blk - cols[i] * ys[i]
                bi = bi - cols[i] * yi[i]
            d_ref[8*r:8*r+8, :B] = blk
            d_ref[8*r:8*r+8, B:] = bi
        if fillers:
            fillers.pop(0)()
    while fillers:
        fillers.pop(0)()


def gram_rows(i, j, nb):
    t = j // 2
    if j == nb - 1:
        return (0, (t * t + 2 * t + 1 + i) * B) if i < 2 else (1, (t * t + t + i - 2) * B)
    return j % 2, (t * t + (j % 2) * t + i) * B


def chol_kernel(first, last, n, planes, spots, *refs):
    begin = first == 0
    info_ref, *refs = refs
    place, myz, myq = here(info_ref)
    if begin:
        slots, (keep_ref, got_ref), refs = refs[:len(spots)], refs[len(spots):len(spots)+2], refs[len(spots)+2:]
    else:
        in_ref, _, _, *refs = refs
    r_keep_ref, r_give_ref, q_ref, *refs = refs
    if begin:
        out_ref, g_ref, t_ref, *refs = refs
        share = g_ref.shape[2]
        for slot, (q, start) in zip(slots, spots):
            for r in range(slot.shape[0]):
                chip = (myz ^ (start + r)) * planes + (myq ^ q)
                for c in range(2):
                    g_ref[chip, place ^ c] = slot[r, c*share:(c+1)*share, :]
        wide = keep_ref.shape[0]
        t_ref[pl.ds(pl.multiple_of(place * wide, wide), wide), :] = keep_ref[...]
        t_ref[pl.ds(pl.multiple_of((1 - place) * wide, wide), wide), :] = got_ref[...]
    r_ref, s_ref, z_ref, d_ref, w_ref, rhs_ref = refs
    nt = z_ref.shape[1]
    nb = n // B
    base = first * B
    ri = lax.broadcasted_iota(jnp.int32, (B, B), 0)
    ci = lax.broadcasted_iota(jnp.int32, (B, B), 1)

    def gram_parts(i, j):
        core, at = gram_rows(i, j, nb)
        share = g_ref.shape[2]
        end, row = at + B, 0
        while at < end:
            chip, off = at // share, at % share
            size = min(share - off, end - at)
            yield row, g_ref[chip, core, off:off+size, :]
            at, row = at + size, row + size

    def load(k, lo, hi):
        if not begin:
            return in_ref[(k-first)*B:(k-first+1)*B, lo-base:hi-base]
        for j in range(lo // B, min(hi, n) // B):
            for row, part in gram_parts(k, j):
                s_ref[k*B+row:k*B+row+part.shape[0], j*B:(j+1)*B] = part
        if hi > n:
            s_ref[k*B:(k+1)*B, n:] = jnp.transpose(t_ref[:, k*B:(k+1)*B])
        return s_ref[k*B:(k+1)*B, lo:hi]

    def current(k, lo, hi):
        return load(k, lo, hi) if k == first else s_ref[k*B-base:(k+1)*B-base, lo-base:hi-base]

    def update(k, i):
        def run():
            lo = i * B
            lhs = split(jnp.transpose(r_ref[k*B-base:(k+1)*B-base, lo:lo+B]))
            lhs = jnp.concatenate([lhs[0], lhs[0], lhs[1]], axis=1)
            upd = jnp.dot(lhs, rhs_ref[k % 2, :, lo-base:], preferred_element_type=F32)
            if i >= last and k == last - 1:
                out_ref[(i-last)*B:(i-last+1)*B, lo-last*B:] = s_ref[lo-base:lo-base+B, lo-base:] - upd
            elif k > first:
                s_ref[lo-base:lo-base+B, lo-base:] = s_ref[lo-base:lo-base+B, lo-base:] - upd
            elif begin:
                for j in range(i, nb):
                    for row, part in gram_parts(i, j):
                        size = part.shape[0]
                        s_ref[lo+row:lo+row+size, j*B:(j+1)*B] = part - upd[row:row+size, (j-i)*B:(j-i+1)*B]
                s_ref[lo:lo+B, n:] = jnp.transpose(t_ref[:, lo:lo+B]) - upd[:, n-lo:]
            else:
                s_ref[lo-base:lo-base+B, lo-base:] = in_ref[lo-base:lo-base+B, lo-base:] - upd
        return run

    fillers = []
    for k in range(first, last):
        lo = k * B
        at = lo - base
        d_ref[:, :B] = current(k, lo, lo + B)
        d_ref[:, B:] = jnp.where(ri == ci, 1.0, 0.0).astype(F32)
        factor_block(d_ref, w_ref, fillers)
        fillers = []
        if k:
            r_ref[at:at+B, :lo] = jnp.zeros((B, lo), F32)
        r_ref[at:at+B, lo:lo+B] = jnp.where(ci >= ri, w_ref[:, :B], 0.0)
        wh, wl = split(w_ref[:, B:])
        w3 = jnp.concatenate([wh, wh, wl], axis=1)
        rh, rl = split(current(k, lo + B, n + nt))
        p = jnp.dot(w3, jnp.concatenate([rh, rl, rh], axis=0), preferred_element_type=F32)
        if k < nb - 1:
            r_ref[at:at+B, lo+B:] = p[:, :n-lo-B]
        z_ref[at:at+B, :] = p[:, n-lo-B:]
        ph, pll = split(p)
        rhs_ref[k % 2, 0:B, lo+B-base:] = ph
        rhs_ref[k % 2, B:2*B, lo+B-base:] = pll
        rhs_ref[k % 2, 2*B:, lo+B-base:] = ph
        if k < nb - 1:
            update(k, k+1)()
            fillers = [update(k, i) for i in range(k+2, nb)]
    for fill in fillers:
        fill()
    tile = r_keep_ref.shape[1]
    r_keep_ref[...] = r_ref[:, pl.ds(pl.multiple_of(place * tile, B), tile)]
    r_give_ref[...] = r_ref[:, pl.ds(pl.multiple_of((1 - place) * tile, B), tile)]
    count = last - first
    coded = [encode(z_ref[k*B:(k+1)*B, :]) for k in range(count)]
    for k in range(count // 2):
        q_ref[k*B:(k+1)*B, :] = join(coded[k][0], coded[k + count // 2][0])
    scales = [join(e, mant) for _, e, mant in coded]
    scales += [jnp.zeros_like(scales[0])] * (8 - count)
    q_ref[count//2*B:, :] = jnp.concatenate(scales, axis=0)


def here(info_ref):
    end = info_ref.shape[0]
    return info_ref[end - 3], info_ref[end - 2], info_ref[end - 1]


def scale_of(e, mant):
    return mant.astype(F32) * jnp.exp2(e.astype(F32)) * (1.0 / (16384.0 * LEVELS))


def encode(x):
    top = jnp.maximum(jnp.max(jnp.abs(x), axis=0, keepdims=True), 1e-30)
    e = jnp.ceil(jnp.log2(top)).astype(jnp.int32)
    mant = jnp.minimum(jnp.ceil(top * jnp.exp2(-e.astype(F32)) * 16384.0) + 1.0, 32767.0).astype(jnp.int32)
    codes = jnp.clip(jnp.round(x * (1.0 / scale_of(e, mant))), -LEVELS, LEVELS)
    return codes.astype(jnp.int32), e, mant


def join(high, low):
    return jnp.bitwise_or(jnp.left_shift(high, 16), jnp.bitwise_and(low, 65535))


def high_low(word):
    return jnp.right_shift(word, 16), jnp.right_shift(jnp.left_shift(word, 16), 16)


def call(kernel, info, args, outs, scratch=(), far=(), cost=0, limit=24, through=0):
    still = pl.BlockSpec(memory_space=pl.ANY)
    kept, made = len(args) - through, len(outs)
    far = tuple(far) + tuple(range(kept, len(args)))
    passed = [jax.ShapeDtypeStruct(arg.shape, arg.dtype) for arg in args[kept:]]
    return pl.pallas_call(
        kernel,
        out_shape=tuple(outs) + tuple(passed),
        grid_spec=pltpu.PrefetchScalarGridSpec(
            num_scalar_prefetch=1,
            grid=(1,),
            in_specs=[
                still if at in far else pl.BlockSpec(arg.shape, lambda i, info, zeros=(0,) * len(arg.shape): zeros)
                for at, arg in enumerate(args)
            ],
            out_specs=tuple(pl.BlockSpec(out.shape, lambda i, info, zeros=(0,) * len(out.shape): zeros) for out in outs) + (still,) * through,
            scratch_shapes=list(scratch),
        ),
        input_output_aliases={1 + kept + i: made + i for i in range(through)},
        compiler_params=pltpu.CompilerParams(vmem_limit_bytes=limit*1024*1024),
        cost_estimate=pl.CostEstimate(flops=cost, bytes_accessed=4*1024*1024, transcendentals=0),
    )(info, *args)


def real(*shape):
    return jax.ShapeDtypeStruct(shape, F32)


def short(*shape):
    return jax.ShapeDtypeStruct(shape, jnp.int16)


def chol_rows(first, last, n, nt, planes, spots, *args):
    vmem = pl.BlockSpec(memory_space=pltpu.VMEM)
    rows = (last - first) * B
    wide = n + nt - first * B
    outs = [real(rows, n // 2), real(rows, n // 2), jax.ShapeDtypeStruct((rows // 2 + 8, nt), jnp.int32)]
    scratch = [
        pltpu.VMEM((rows, n), F32),
        pltpu.VMEM((n - first * B, wide), F32),
        pltpu.VMEM((rows, nt), F32),
        pltpu.VMEM((B, 2*B), F32),
        pltpu.VMEM((B, 2*B), F32),
        pltpu.VMEM((2, 3*B, wide), BF),
    ]
    specs = [pl.BlockSpec(memory_space=pltpu.SMEM)] + [vmem] * (len(args) - 1)
    if first == 0:
        outs.append(real(n - last * B, n + nt - last * B))
        share = args[1].shape[1] // 2
        scratch = [pltpu.VMEM((planes * ZS, 2, share, B), F32), pltpu.VMEM((nt, n), F32)] + scratch
    else:
        specs[2:] = [pl.BlockSpec(memory_space=pl.ANY)] * 2
    return pl.pallas_call(
        lambda *refs: chol_kernel(first, last, n, planes, spots, *refs),
        out_shape=tuple(outs),
        in_specs=specs,
        out_specs=(vmem,) * len(outs),
        scratch_shapes=scratch,
        compiler_params=pltpu.CompilerParams(vmem_limit_bytes=26*1024*1024),
        cost_estimate=pl.CostEstimate(flops=30*n*n*n // 2, bytes_accessed=4*rows*n, transcendentals=0),
    )(*args)


def factor_kernel(info_ref, *refs):
    tiles, out_ref, token_ref = refs[:-2], refs[-2], refs[-1]
    token_ref[...] = jnp.zeros(token_ref.shape, F32)
    place, myz, myq = here(info_ref)
    row = 0
    for at in range(0, len(tiles), 2):
        rows = tiles[at].shape[0]
        out_ref[place, row:row+rows, :] = tiles[at][...]
        out_ref[1 - place, row:row+rows, :] = tiles[at+1][...]
        row += rows


DIMS = (((0,), (0,)), ((), ()))


def pivot_kernel(info_ref, own_ref, other_ref, a_ref, *refs):
    slots, g_ref = refs[:-1], refs[-1]
    live, tile = other_ref.shape
    n = a_ref.shape[1]
    place, myz, myq = here(info_ref)
    rows = lax.broadcasted_iota(jnp.int32, (live, B), 0)
    zero = jnp.zeros((live, B), BF)
    per = tile // B
    for half, ref in ((place, own_ref), (1 - place, other_ref)):
        for j in range(per):
            end = info_ref[half * per + j]
            at = pl.multiple_of(half * tile + j * B, B)
            a_ref[:, pl.ds(at, B)] = jnp.where(rows < end, ref[:, j*B:(j+1)*B], zero)
    nb = n // B
    for core in range(2):
        @pl.when(place == core)
        def _():
            runs = [(j, 0, j + 1) for j in range(core, nb - 1, 2)] + [(nb - 1, 0, 2) if core == 0 else (nb - 1, 2, nb)]
            for j, low, high in runs:
                at = gram_rows(low, j, nb)[1]
                g_ref[at:at+(high-low)*B, :] = lax.dot_general(
                    a_ref[:, low*B:high*B], a_ref[:, j*B:(j+1)*B], DIMS, preferred_element_type=F32
                )
    used = nb * (nb + 1) // 4 * B
    if used < g_ref.shape[0]:
        g_ref[used:, :] = jnp.zeros((g_ref.shape[0] - used, B), F32)
    share = slots[0].shape[0] // ZS
    for q, slot in enumerate(slots):
        for z in range(ZS):
            at = pl.multiple_of((z * len(slots) + (myq ^ q)) * share, 8)
            slot[z*share:(z+1)*share, :] = g_ref[pl.ds(at, share), :]
        if q:
            slot[ZS*share:, :] = jnp.full((8, B), info_ref[info_ref.shape[0] - 4], jnp.int32).astype(F32)


def pivot_plane_kernel(planes, info_ref, own_ref, *refs):
    got, slots = refs[:planes-1], refs[2*(planes-1):2*(planes-1)+ZS]
    share = own_ref.shape[0] // ZS
    place, myz, myq = here(info_ref)
    parent = info_ref[info_ref.shape[0] - 4]
    theirs = [jnp.broadcast_to(ref[ZS*share:ZS*share+1, :], (share, B)) for ref in got]
    for r, slot in enumerate(slots):
        at = pl.multiple_of((myz ^ r) * share, 8)
        own = own_ref[pl.ds(at, share), :]
        parts = [ref[pl.ds(at, share), :] for ref in got]
        for p in range(NPAR):
            total = jnp.where(parent == p, own, 0.0)
            for part, their in zip(parts, theirs):
                total = total + jnp.where(their == p, part, 0.0)
            slot[p*share:(p+1)*share, :] = total


def pivot_line_kernel(info_ref, own_ref, *refs):
    got, outs = refs[:ZS-1], refs[-2:]
    share = own_ref.shape[0] // NPAR
    place, myz, myq = here(info_ref)
    for out, p in zip(outs, (place, 1 - place)):
        at = pl.ds(pl.multiple_of(p * share, 8), share)
        total = own_ref[at, :]
        for ref in got:
            total = total + ref[at, :]
        out[...] = total


def trail_kernel(info_ref, a_ref, trail_ref, *refs):
    slots, (t_ref, own_ref, done) = refs[:-3], refs[-3:]
    live, n = a_ref.shape
    wide = trail_ref.shape[2] // ZS
    copies = [
        pltpu.make_async_copy(trail_ref.at[0, pl.ds(0, live), pl.ds(z * wide, wide)], own_ref.at[z], done.at[z]) for z in range(ZS)
    ]
    for copy in copies:
        copy.start()
    place, myz, myq = here(info_ref)
    rows = lax.broadcasted_iota(jnp.int32, (live, B), 0)
    zero = jnp.zeros((live, B), BF)
    per = trail_ref.shape[2] // B
    group = per // ZS
    width = slots[0].shape[0] // ZS
    scales = [[] for _ in slots]
    for z in range(ZS):
        copies[z].wait()
        cols = []
        for h in range(group):
            end = info_ref[n // B + place * per + z * group + h]
            cols.append(jnp.where(rows < end, own_ref[z, :, h*B:(h+1)*B], zero))
        t_ref[z % 2] = lax.dot_general(jnp.concatenate(cols, axis=1), a_ref[...], DIMS, preferred_element_type=F32)
        for q, slot in enumerate(slots):
            at = pl.multiple_of((myq ^ q) * width, width)
            part = t_ref[z % 2, pl.ds(at, width), :]
            if q:
                part, e, mant = encode(part)
                scales[q].append((e, mant))
            slot[z*width:(z+1)*width, :] = part.astype(slot.dtype)
    for q, slot in enumerate(slots):
        if q:
            spare = [jnp.full((1, n), info_ref[info_ref.shape[0] - 4], jnp.int32)]
            write_scales(slot, ZS * width, [e for e, _ in scales[q]] + [m for _, m in scales[q]] + spare)


def write_scales(slot, at, rows):
    rows = rows + [jnp.zeros_like(rows[0])] * (16 - len(rows))
    slot[at:at+16, :] = jnp.concatenate(rows, axis=0).astype(jnp.int16)


def row_of(tile, index):
    rows = lax.broadcasted_iota(jnp.int32, tile.shape, 0)
    return jnp.sum(jnp.where(rows == index, tile, 0), axis=0, keepdims=True)


def trail_plane_kernel(info_ref, own_ref, *refs):
    got, slots = refs[:-ZS], refs[-ZS:]
    width = own_ref.shape[0] // ZS
    place, myz, myq = here(info_ref)
    parent = info_ref[info_ref.shape[0] - 4]
    tiles = [ref[ZS*width:, :].astype(jnp.int32) for ref in got]
    for r, slot in enumerate(slots):
        z = myz ^ r
        at = pl.multiple_of(z * width, width)
        own = own_ref[pl.ds(at, width), :]
        parts = [ref[pl.ds(at, width), :].astype(jnp.int32).astype(F32) for ref in got]
        steps = [scale_of(row_of(tile, z), row_of(tile, ZS + z)) for tile in tiles]
        scales = []
        for p in range(NPAR):
            total = jnp.where(parent == p, own, 0.0)
            for part, step, tile in zip(parts, steps, tiles):
                total = total + part * jnp.where(tile[2*ZS:2*ZS+1, :] == p, step, 0.0)
            if r:
                total, e, mant = encode(total)
                scales.append((e, mant))
            slot[p*width:(p+1)*width, :] = total.astype(slot.dtype)
        if r:
            write_scales(slot, NPAR * width, [e for e, _ in scales] + [m for _, m in scales])


def trail_line_kernel(info_ref, own_ref, *refs):
    got, outs = refs[:-2], refs[-2:]
    width = own_ref.shape[0] // NPAR
    place, myz, myq = here(info_ref)
    tiles = [ref[NPAR*width:, :].astype(jnp.int32) for ref in got]
    for out, p in zip(outs, (place, 1 - place)):
        at = pl.ds(pl.multiple_of(p * width, width), width)
        total = own_ref[at, :]
        for ref, tile in zip(got, tiles):
            total = total + ref[at, :].astype(jnp.int32).astype(F32) * scale_of(row_of(tile, p), row_of(tile, NPAR + p))
        out[...] = total


def unpack_kernel(spots, info_ref, *refs):
    o_ref = refs[-1]
    planes = 4
    words, scales = refs[:len(spots)], refs[len(spots):2*len(spots)]
    place, myz, myq = here(info_ref)
    zs, rows, lanes = words[0].shape
    found = {(q, start + r): (at, r) for at, (q, start) in enumerate(spots) for r in range(words[at].shape[0])}
    half = lanes // 2
    lane = lax.broadcasted_iota(jnp.int32, (rows, lanes), 1)
    which = lax.broadcasted_iota(jnp.int32, (8, lanes), 0)
    blocks = pl.num_programs(0)
    odd = (myq & 1) == 1

    def values(q, r):
        at, r = found[q, r]
        steps = scale_of(*high_low(scales[at][r]))
        picked = [jnp.sum(jnp.where(which == pl.program_id(0) + h * blocks, steps, 0.0), axis=0, keepdims=True) for h in (0, 1)]
        return [v.astype(F32) * step for v, step in zip(high_low(words[at][r]), picked)]

    for q in range(0, planes, 2):
        for r in range(zs):
            at = pl.multiple_of(((myz ^ r) * planes + ((myq ^ q) & 2)) * half, lanes)
            for h, (a, b) in enumerate(zip(values(q, r), values(q + 1, r))):
                a, b = jnp.where(odd, b, a), jnp.where(odd, a, b)
                o_ref[0, 0, h, :, pl.ds(at, lanes)] = jnp.where(lane < half, a, pltpu.roll(b, half, 1))
                o_ref[1, 0, h, :, pl.ds(at, lanes)] = jnp.where(lane < half, pltpu.roll(a, half, 1), b)


def unpack(info, slots, spots, part, parts, *behind):
    zs, rows, lanes = slots[0].shape
    rows -= 8
    wide = 4 * zs * lanes // 2
    blocks = rows // B
    args = list(slots) * 2
    specs = [pl.BlockSpec((x.shape[0], B, lanes), lambda k, info: (0, k, 0)) for x in slots]
    specs += [pl.BlockSpec((x.shape[0], 8, lanes), lambda k, info: (0, rows // 8, 0)) for x in slots]
    for extra in behind:
        args.append(extra)
        specs.append(pl.BlockSpec(memory_space=pl.ANY))
    return pl.pallas_call(
        lambda *refs: unpack_kernel(spots, *refs),
        out_shape=real(NPAR, parts, 2, rows, wide),
        grid_spec=pltpu.PrefetchScalarGridSpec(
            num_scalar_prefetch=1,
            grid=(blocks,),
            in_specs=specs,
            out_specs=pl.BlockSpec((NPAR, 1, 2, B, wide), lambda k, info: (0, part, 0, k, 0)),
        ),
        input_output_aliases={2 * len(slots) + 1: 0} if part else {},
        compiler_params=pltpu.CompilerParams(vmem_limit_bytes=32*1024*1024),
        cost_estimate=pl.CostEstimate(flops=0, bytes_accessed=20*rows*wide, transcendentals=0),
    )(info, *args)


def unpack_plain(q):
    chips, rows, lanes = q.shape
    rows -= 8
    blocks = rows // B
    step = scale_of(*high_low(q[:, rows:rows+2*blocks])).reshape(chips, 2, blocks, 1, lanes)
    z = jnp.stack(high_low(q[:, :rows]), axis=1).astype(F32).reshape(chips, 2, blocks, B, lanes) * step
    z = z.reshape(chips, 2 * rows, NPAR, lanes // NPAR)
    return jnp.transpose(z, (2, 1, 0, 3)).reshape(NPAR, 2 * rows, chips * lanes // NPAR)


def shards(count, piv_cols, trail_cols, row_end, parent_of):
    place = lax.axis_index("front")
    me = lax.axis_index("sub")
    planes = count // ZS
    myz, myq = me // planes, me % planes
    tile_pivot, tile_trail = piv_cols.shape[2], trail_cols.shape[2]
    n = NPAR * tile_pivot
    width = tile_trail // count
    nb = n // B
    share = -(-(nb * (nb + 1) // 4 * B) // (8 * count)) * 8

    def flip(x, mask):
        return lax.ppermute(x, "sub", [(i, i ^ mask) for i in range(count)])

    def over_plane(slots):
        return [flip(x, q) for q, x in enumerate(slots) if q]

    def over_line(slots):
        return [flip(x, r * planes) for r, x in enumerate(slots) if r]

    def everywhere(x):
        line = jnp.stack([x] + over_line([x] * ZS))
        if planes != 4:
            return [line] + over_plane([line] * planes)
        one, two = flip(line, 1), flip(line, 2)
        return [line, one, two, flip(one[:ZS//2], 2), flip(two[ZS//2:], 1)]

    spots = [(q, 0) for q in range(planes)]
    if planes == 4:
        spots = spots + [(3, ZS // 2)]

    own_piv = piv_cols[0, :LIVE]
    other_piv = lax.ppermute(own_piv, "front", SWAP)
    info = jnp.concatenate([row_end[0], parent_of, jnp.stack([place, myz, myq]).astype(jnp.int32)])

    outs = [jax.ShapeDtypeStruct((LIVE, n), BF), real(ZS * share, B)] + [real(ZS * share + 8, B)] * (planes - 1)
    masked, *slots = call(
        pivot_kernel, info, (own_piv, other_piv), outs,
        [pltpu.VMEM((count * share, B), F32)], cost=LIVE*n*n,
    )
    got = over_plane(slots)
    outs = [real(ZS * width, n)] + [short(ZS * width + 16, n)] * (planes - 1)
    trails = call(
        trail_kernel, info, (masked, trail_cols), outs,
        [pltpu.VMEM((2, planes * width, n), F32), pltpu.VMEM((ZS, LIVE, tile_trail // ZS), BF), pltpu.SemaphoreType.DMA((ZS,))],
        far=(1,), cost=2*LIVE*n*tile_trail, limit=32,
    )
    out = call(
        lambda *refs: pivot_plane_kernel(planes, *refs), info, (slots[0], *got, *trails[1:]), [real(NPAR * share, B)] * ZS,
        through=planes-1,
    )
    slots, trails = out[:ZS], [trails[0], *out[ZS:]]
    got_trails = over_plane(trails)
    ahead = got_trails[:2]
    keep, give = call(
        pivot_line_kernel, info, (slots[0], *over_line(slots), *ahead), [real(share, B)] * 2, far=range(ZS, ZS + len(ahead))
    )
    grams = everywhere(jnp.concatenate([keep, lax.ppermute(give, "front", SWAP)], axis=0))

    outs = [real(NPAR * width, n)] + [short(NPAR * width + 16, n)] * (ZS - 1)
    trails = call(trail_plane_kernel, info, (trails[0], *got_trails), outs)
    keep, give = call(trail_line_kernel, info, (trails[0], *over_line(trails)), [real(width, n)] * 2)
    got = lax.ppermute(give, "front", SWAP)

    def gather(codes):
        theirs = lax.ppermute(codes, "front", SWAP)
        return jnp.where(
            place == 0,
            jnp.concatenate([codes[:, :width], theirs[:, :width]], axis=1),
            jnp.concatenate([theirs[:, width:], codes[:, width:]], axis=1),
        )

    def in_order(slots):
        every = jnp.stack(slots)
        every = jnp.take(jnp.take(every, jnp.arange(planes) ^ myq, axis=0), jnp.arange(ZS) ^ myz, axis=1)
        return jnp.swapaxes(every, 0, 1).reshape((count,) + every.shape[2:])

    r_keep, give, codes, rest = chol_rows(0, nb // 2, n, NPAR * width, planes, spots, info, *grams, keep, got)
    words, give = lax.optimization_barrier((gather(codes), give))
    tiles = [r_keep, lax.ppermute(give, "front", SWAP)]
    first = everywhere(words)
    r_keep, give, codes = chol_rows(nb // 2, nb, n, NPAR * width, planes, spots, info, rest, words, tiles[1])
    tiles += [r_keep, lax.ppermute(give, "front", SWAP)]
    second = everywhere(gather(codes))
    r_pivot, token = call(factor_kernel, info, tiles, [real(NPAR, n, tile_pivot), real(8, B)], limit=32)
    if 2 * width == B and planes == 4:
        r_trail = unpack(info, first, spots, 0, 2)
        r_trail = unpack(info, second, spots, 1, 2, r_trail, token).reshape(NPAR, n, -1)
    else:
        r_trail = jnp.concatenate([unpack_plain(in_order(first)), unpack_plain(in_order(second))], axis=1)
    return (r_pivot, r_trail)


def solution(mesh):
    count = mesh.shape["sub"]
    return jax.shard_map(
        lambda *args: shards(count, *args),
        mesh=mesh,
        in_specs=(P("sub", None, "front"), P("sub", None, "front"), P("sub", None), P("sub")),
        out_specs=(P(None, None, "front"), P(None, None, "front")),
        check_vma=False,
    )
```
